256 devices in a mesh: pen: 32 (over y, z_lo, core), chan: 8 (over x, z_hi).
Axes of the slice: x: 4, y: 4, z: 8 (z_hi: 2, z_lo: 4; z = z_hi * 4 + z_lo), core: 2. Of those that a mesh axis runs over, the one named last changes fastest.
Arguments:
- latents: bfloat16 [384, 1440, 256], P('pen', 'chan'), may hold values from -6 to 6
- norm_gain: float32 [256], replicated, may hold values from 0.1 to 1.9
- weight_in: bfloat16 [1024, 256], P(('pen', 'chan')), may hold values from -0.375 to 0.375
- weight_out: bfloat16 [1024, 256], P(('pen', 'chan')), may hold values from -0.1875 to 0.1875
- filter_first: bfloat16 [2, 8, 32, 32], P(None, 'chan'), may hold values from -0.75 to 0.75
- filter_second: bfloat16 [2, 8, 32, 32], P(None, 'chan'), may hold values from -0.75 to 0.75
- cotangent: bfloat16 [384, 1440, 256], P('pen', 'chan'), may hold values from -6 to 6
Outputs:
- block_output: bfloat16 [384, 1440, 256], P('pen', 'chan')
- grad_latents: bfloat16 [384, 1440, 256], P('pen', 'chan')
- grad_weight_in: float32 [1024, 256], P(('pen', 'chan'))
- grad_weight_out: float32 [1024, 256], P(('pen', 'chan'))
- grad_filter_first: float32 [2, 8, 32, 32], P(None, 'chan')
- grad_filter_second: float32 [2, 8, 32, 32], P(None, 'chan')
The draws below stay inside these ranges and needn't reach their ends.
All inputs are finite; a program needn't handle non-finite values.
Results may differ from the reference program's by a relative error of at most 0.015.
The reference program's roundings to bfloat16 on the way count: a program that leaves them out, or rounds other values in their place, can miss the bound.
Values may be sent and summed in bfloat16 or wider, within the bound.
A program may use at most 128 MiB of HBM per device.

```python
import math
import jax
import jax.numpy as jnp
from jax import lax

NLAT = 384
NLON = 1440
KLON = 384
C = 256
NB = 8
BS = 32
HID = 1024


def level_of(key, extent, pieces, smallest, high):
    factor_of = 1.0
    for dim, blocks in pieces:
        draws = jax.random.uniform(jax.random.fold_in(jax.random.fold_in(key, 6), dim), (blocks,), jnp.float32, smallest / len(pieces), high / len(pieces))
        factor_of = factor_of * jnp.repeat(jnp.exp(draws), extent[dim] // blocks).reshape((-1,) + (1,) * (len(extent) - 1 - dim))
    return factor_of


def bell_draw(own_key, dims, scale, bound, cuts=(), kind=jnp.bfloat16):
    level = level_of(own_key, dims, cuts, -0.22, 0.18) if cuts else 1.0
    result = jax.random.normal(own_key, dims, jnp.float32) * scale * level
    return jnp.minimum(jnp.maximum(result, -bound), bound).astype(kind)


def setup_inputs(seed: int = 0) -> dict:
    key_list = jax.random.split(jax.random.key(seed), 8)
    return {
        "latents": bell_draw(key_list[0], (NLAT, NLON, C), 1.0, 6.0, ((0, 32), (1, 8))),
        "norm_gain": jnp.clip(1.0 + 0.18 * jax.random.normal(key_list[1], (C,), jnp.float32), 0.1, 1.9),
        "weight_in": bell_draw(key_list[2], (HID, C), C ** -0.5, 0.375, ((0, 256),)),
        "weight_out": bell_draw(key_list[3], (HID, C), HID ** -0.5, 0.1875, ((0, 256),)),
        "filter_first": bell_draw(key_list[4], (2, NB, BS, BS), (2 * BS) ** -0.5, 0.75, ((1, 8),)),
        "filter_second": bell_draw(key_list[5], (2, NB, BS, BS), (2 * BS) ** -0.5, 0.75, ((1, 8),)),
        "cotangent": bell_draw(key_list[6], (NLAT, NLON, C), 1.0, 6.0, ((0, 32), (1, 8))),
    }


def zonal_tables():
    column = jnp.arange(NLON, dtype=jnp.int32)[:, None]
    number = jnp.arange(KLON, dtype=jnp.int32)[None, :]
    phase = (column * number % NLON).astype(jnp.float32) * (2.0 * math.pi / NLON)
    factor = 1.0 / math.sqrt(NLON)
    forward = jnp.concatenate([jnp.cos(phase), -jnp.sin(phase)], axis=1) * factor
    weights = jnp.where(number == 0, 1.0, 2.0).astype(jnp.float32)
    inverse = jnp.concatenate([jnp.cos(phase) * weights, -jnp.sin(phase) * weights], axis=1).T * factor
    return (forward.astype(jnp.bfloat16), inverse.astype(jnp.bfloat16))

def meridian_table():
    row_mode = jnp.arange(NLAT, dtype=jnp.int32)[:, None]
    row_lat = jnp.arange(NLAT, dtype=jnp.int32)[None, :]
    phase = (row_mode * row_lat % NLAT).astype(jnp.float32) * (2.0 * math.pi / NLAT)
    factor = 1.0 / math.sqrt(NLAT)
    real_part = jnp.cos(phase) * factor
    imag_part = -jnp.sin(phase) * factor
    upper = jnp.stack([real_part, -imag_part], axis=1)
    lower = jnp.stack([imag_part, real_part], axis=1)
    return jnp.stack([upper, lower], axis=0).astype(jnp.bfloat16)

def normalize(values, norm_gain):
    centred = values - lax.optimization_barrier(jnp.mean(values, axis=-1, keepdims=True))
    spread = lax.optimization_barrier(jnp.mean(centred * centred, axis=-1, keepdims=True))
    return centred * lax.rsqrt(spread + 1e-05) * norm_gain

def complex_stack(matrix):
    return jnp.stack([jnp.stack([matrix[0], matrix[1]]), jnp.stack([-matrix[1], matrix[0]])])

def block_forward(spectra, first, second):
    first_c = complex_stack(first).astype(jnp.float32)
    second_c = complex_stack(second).astype(jnp.float32)
    first_act = jnp.einsum('prba,pqbae->qrbe', spectra.astype(jnp.float32), first_c)
    first_hidden = jax.nn.gelu(first_act).astype(jnp.bfloat16)
    second_act = jnp.einsum('prba,pqbae->qrbe', first_hidden.astype(jnp.float32), second_c)
    shrunk = (second_act - 0.1 * jnp.tanh(second_act * 10.0)).astype(jnp.bfloat16)
    return (shrunk, (first_act, first_hidden, second_act))

def fold_grad(outer):
    return jnp.stack([outer[0, 0] + outer[1, 1], outer[0, 1] - outer[1, 0]])

def block_backward(spectra, first, second, stored, d_shrunk):
    first_act, first_hidden, second_act = stored
    first_c = complex_stack(first).astype(jnp.float32)
    second_c = complex_stack(second).astype(jnp.float32)
    slope = jnp.tanh(second_act * 10.0)
    d_second = (d_shrunk.astype(jnp.float32) * slope * slope).astype(jnp.bfloat16)
    outer_two = jnp.einsum('prba,qrbe->pqbae', first_hidden.astype(jnp.float32), d_second.astype(jnp.float32))
    d_hidden = jnp.einsum('qrbe,pqbae->prba', d_second.astype(jnp.float32), second_c)
    unused, pull_gelu = jax.vjp(jax.nn.gelu, first_act)
    d_first = pull_gelu(d_hidden)[0].astype(jnp.bfloat16)
    outer_one = jnp.einsum('prba,qrbe->pqbae', spectra.astype(jnp.float32), d_first.astype(jnp.float32))
    d_spectra = jnp.einsum('qrbe,pqbae->prba', d_first.astype(jnp.float32), first_c).astype(jnp.bfloat16)
    return (d_spectra, fold_grad(outer_one), fold_grad(outer_two))

def reference(latents, norm_gain, weight_in, weight_out, filter_first, filter_second, cotangent):
    forward_zonal, inverse_zonal = zonal_tables()
    meridian = meridian_table()
    meridian_f = meridian.astype(jnp.float32)
    normed_f, pull_norm = jax.vjp(lambda values: normalize(values, norm_gain), latents.astype(jnp.float32))
    normed = normed_f.astype(jnp.bfloat16)

    def mlp_row(carry, rows):
        normed_row, grad_row = rows
        pre_act = jnp.dot(normed_row, weight_in.T, preferred_element_type=jnp.float32)
        hidden = jax.nn.gelu(pre_act).astype(jnp.bfloat16)
        column_mix = jnp.dot(hidden, weight_out, preferred_element_type=jnp.float32)
        d_hidden = jnp.dot(grad_row, weight_out.T, preferred_element_type=jnp.float32)
        unused, pull_gelu = jax.vjp(jax.nn.gelu, pre_act)
        d_pre = pull_gelu(d_hidden)[0].astype(jnp.bfloat16)
        d_column = jnp.dot(d_pre, weight_in, preferred_element_type=jnp.float32)
        sum_in = carry[0] + jnp.dot(d_pre.T, normed_row, preferred_element_type=jnp.float32)
        sum_out = carry[1] + jnp.dot(hidden.T, grad_row, preferred_element_type=jnp.float32)
        return ((sum_in, sum_out), (column_mix, d_column))
    zeros_init = jnp.zeros((HID, C), jnp.float32)
    (grad_weight_in, grad_weight_out), (column_mix, d_column) = lax.scan(mlp_row, (zeros_init, zeros_init), (normed, cotangent))
    zonal_modes = jnp.einsum('ljc,jq->lqc', normed.astype(jnp.float32), forward_zonal.astype(jnp.float32)).astype(jnp.bfloat16)
    zonal_split = zonal_modes.reshape(NLAT, 2, KLON, C).astype(jnp.float32)
    spectrum = jnp.einsum('qmpi,ipkc->qmkc', meridian_f, zonal_split).astype(jnp.bfloat16)
    blocks = spectrum.reshape(2, NLAT * KLON, NB, BS)
    shrunk, stored = block_forward(blocks, filter_first, filter_second)
    shrunk_split = shrunk.reshape(2, NLAT, KLON, C).astype(jnp.float32)
    inverse_lat = jnp.einsum('qmpi,qmkc->ipkc', meridian_f, shrunk_split).astype(jnp.bfloat16)
    inverse_lat = inverse_lat.reshape(NLAT, 2 * KLON, C).astype(jnp.float32)
    spatial = jnp.einsum('lqc,qj->ljc', inverse_lat, inverse_zonal.astype(jnp.float32)).astype(jnp.bfloat16)
    block_output = (latents.astype(jnp.float32) + spatial.astype(jnp.float32) + column_mix).astype(jnp.bfloat16)
    d_inverse = jnp.einsum('ljc,qj->lqc', cotangent.astype(jnp.float32), inverse_zonal.astype(jnp.float32)).astype(jnp.bfloat16)
    d_inverse = d_inverse.reshape(NLAT, 2, KLON, C).astype(jnp.float32)
    d_shrunk = jnp.einsum('qmpi,ipkc->qmkc', meridian_f, d_inverse).astype(jnp.bfloat16)
    d_blocks, grad_filter_first, grad_filter_second = block_backward(blocks, filter_first, filter_second, stored, d_shrunk.reshape(blocks.shape))
    d_split = d_blocks.reshape(2, NLAT, KLON, C).astype(jnp.float32)
    d_zonal = jnp.einsum('qmpi,qmkc->ipkc', meridian_f, d_split).astype(jnp.bfloat16)
    d_zonal = d_zonal.reshape(NLAT, 2 * KLON, C).astype(jnp.float32)
    d_spatial = jnp.einsum('lqc,jq->ljc', d_zonal, forward_zonal.astype(jnp.float32)).astype(jnp.bfloat16)
    d_normed = d_column + d_spatial.astype(jnp.float32)
    grad_latents = (cotangent.astype(jnp.float32) + pull_norm(d_normed)[0]).astype(jnp.bfloat16)
    return (block_output, grad_latents, grad_weight_in, grad_weight_out, grad_filter_first, grad_filter_second)
```

```python
import functools
import math

import jax
import jax.numpy as jnp
import ml_dtypes
import numpy as np
from jax import lax
from jax.experimental import pallas as pl
from jax.experimental.pallas import tpu as pltpu
from jax.sharding import PartitionSpec as P

MESH = pl.DeviceIdType.MESH
NLON, KLON, NLAT = 1440, 384, 384
SEG = 180
PAD = 192
RANK = 128
LAT = 12
NK = 12
GELU_C = math.sqrt(2.0 / math.pi)
F32, BF16 = jnp.float32, jnp.bfloat16


def as_bf16(values):
    return np.asarray(values, np.float32).astype(ml_dtypes.bfloat16)


@functools.lru_cache(None)
def tables():
    j = np.arange(NLON)[:, None]
    k = np.arange(KLON)[None, :]
    a = 2.0 * np.pi * ((j * k) % NLON) / NLON
    full = np.concatenate([np.cos(a), -np.sin(a)], axis=1) / math.sqrt(NLON)
    left, _, _ = np.linalg.svd(full[:SEG], full_matrices=False)
    basis = left[:, :RANK]
    expand = np.stack([basis.T @ full[s * SEG : (s + 1) * SEG] for s in range(8)])
    expand = expand.reshape(8, RANK, 2, 32, NK).transpose(3, 2, 4, 0, 1).reshape(768, 8 * RANK)
    basis_pad = np.zeros((PAD, RANK))
    basis_pad[:SEG] = basis
    s = np.arange(32)
    w32 = np.exp(-2j * np.pi * np.outer(s, s) / 32)
    l = np.arange(12)
    w12 = np.exp(-2j * np.pi * np.outer(l, l) / 12)

    def real_form(w):
        return np.stack(
            [np.stack([w.real, -w.imag], axis=1), np.stack([w.imag, w.real], axis=1)]
        )

    first = np.einsum("qmps,kl->qmkspl", real_form(w32), np.eye(NK)).reshape(768, 768)
    second = np.einsum("qmpl,cd->plcqmd", real_form(w12), np.eye(32)).reshape(768, 768)
    twiddle = np.exp(-2j * np.pi * np.outer(s, l) / 384) / math.sqrt(NLAT)
    twiddle = np.repeat(np.repeat(twiddle, NK, axis=0), 32, axis=1)
    return dict(
        basis=as_bf16(basis_pad),
        expand=as_bf16(expand),
        first=as_bf16(first),
        first_t=as_bf16(first.T),
        second=as_bf16(second),
        second_t=as_bf16(second.T),
        tw_re=np.asarray(twiddle.real, np.float32),
        tw_im=np.asarray(twiddle.imag, np.float32),
    )


CONSTS = ("basis", "expand", "first", "first_t", "second", "second_t", "tw_re", "tw_im")


def dot(a, b, ca=1, cb=0):
    return lax.dot_general(a, b, (((ca,), (cb,)), ((), ())), preferred_element_type=F32)


def gelu_parts(v):
    v2 = v * v
    t = jnp.tanh(v * (GELU_C + (GELU_C * 0.044715) * v2))
    half = 0.5 + 0.5 * t
    value = v * half
    slope = half + (0.5 * v) * (1.0 - t * t) * (GELU_C + (3.0 * GELU_C * 0.044715) * v2)
    return value, slope


class Push:
    def __init__(self, send_sem, recv_sem):
        self.send_sem, self.recv_sem, self.copies = send_sem, recv_sem, []

    def start(self, src, dst, device):
        n = len(self.copies)
        copy = pltpu.make_async_remote_copy(
            src_ref=src,
            dst_ref=dst,
            send_sem=self.send_sem.at[n],
            recv_sem=self.recv_sem.at[n],
            device_id=device,
            device_id_type=MESH,
        )
        copy.start()
        self.copies.append(copy)

    def wait_recv(self):
        for copy in self.copies:
            copy.wait_recv()

    def wait_send(self):
        for copy in self.copies:
            copy.wait_send()


def kernel(*refs):
    (lat_ref, gain_ref, win_ref, wout_ref, ff_ref, fs_ref, cot_ref) = refs[:7]
    const_hbm = refs[7 : 7 + len(CONSTS)]
    refs = refs[7 + len(CONSTS) :]
    (bo_ref, gl_ref, gwi_ref, gwo_ref, gff_ref, gfs_ref) = refs[:6]
    refs = refs[6:]
    const = refs[: len(CONSTS)]
    refs = refs[len(CONSTS) :]
    (normed_s, cot_s, send1, recv1, send2, recv2, send3, recv3, send4, recv4) = refs[:10]
    (cm_s, dc_s, zsrc, zbuf, pk, wfull, gacc, gsc, grc, gsx, grx, gsz, grz) = refs[10:23]
    (fbuf, frc, fry, frz) = refs[23:27]
    (const_sem, s1s, s1r, s2s, s2r, s3s, s3r, s4s, s4r) = refs[27:36]
    (wzs, wzr, wxs, wxr, wcs, wcr, gzs, gzr, gxs, gxr, gcs, gcr) = refs[36:48]
    (fcs, fcr, fys, fyr, fzs, fzr) = refs[48:54]
    V, expand, first, first_t, second, second_t, tw_re, tw_im = const

    pen = lax.axis_index("pen")
    chan = lax.axis_index("chan")
    x, zhi = chan // 2, lax.rem(chan, 2)
    y, zlo, core = pen // 8, lax.rem(pen // 2, 4), lax.rem(pen, 2)
    z = zhi * 4 + zlo
    xy = x * 4 + y

    def device(x_, y_, z_, core_):
        return (y_ * 8 + lax.rem(z_, 4) * 2 + core_, x_ * 2 + z_ // 4)

    chan_peers = [(pen, lax.rem(chan + d, 8)) for d in range(1, 8)]
    pen_peers = [(lax.rem(pen + d, 32), chan) for d in range(1, 32)]
    z_index = [lax.rem(z + d, 8) for d in range(1, 8)]
    z_peers = [device(x, y, i, core) for i in z_index]
    xy_index = [lax.rem(xy + d, 16) for d in range(1, 16)]
    xy_peers = [device(i // 4, lax.rem(i, 4), z, core) for i in xy_index]
    sibling = device(x, y, z, 1 - core)
    y_peers = [device(x, lax.rem(y + d, 4), z, core) for d in range(1, 4)]
    zlo_peers = [device(x, y, zhi * 4 + lax.rem(zlo + d, 4), core) for d in range(1, 4)]

    loads = []
    for n, (src, dst) in enumerate(zip(const_hbm, const)):
        load = pltpu.make_async_copy(src, dst, const_sem.at[n])
        load.start()
        loads.append(load)
    loads = dict(zip(CONSTS, loads))

    barrier = pltpu.get_barrier_semaphore()
    greeted = chan_peers + pen_peers + z_peers + xy_peers
    for peer in greeted:
        pl.semaphore_signal(barrier, inc=1, device_id=peer, device_id_type=MESH)

    zsrc[0:4, :] = win_ref[...].astype(F32)
    zsrc[4:8, :] = wout_ref[...].astype(F32)
    zbuf[z] = zsrc[...]
    normed_s[:, 176:192, :] = jnp.zeros((LAT, 16, 256), BF16)
    cot_s[:, 176:192, :] = jnp.zeros((LAT, 16, 256), BF16)
    pl.semaphore_wait(barrier, len(greeted))

    w_z = Push(wzs, wzr)
    for peer in z_peers:
        w_z.start(zsrc, zbuf.at[z], peer)

    loads["basis"].wait()

    def compress(rows, slot, l):
        coded = dot(rows, V[...], 0, 0).astype(BF16)
        send1[slot, :, l] = coded.reshape(8, 32, RANK)

    def cot_row(l, carry):
        cot_s[l, 0:SEG] = cot_ref[l]
        compress(cot_s[l], 1, l)
        return carry

    lax.fori_loop(0, LAT, cot_row, 0)
    ex1 = [None, None]
    ex1[1] = Push(s1s.at[1], s1r.at[1])
    for d, peer in enumerate(chan_peers):
        ex1[1].start(send1.at[1, peer[1]], recv1.at[1, chan], peer)
    recv1[1, chan] = send1[1, chan]

    w_z.wait_recv()
    pk[0] = jnp.concatenate([zbuf[i, 0:4] for i in range(8)], axis=0).astype(BF16)
    pk[1] = jnp.concatenate([zbuf[i, 4:8] for i in range(8)], axis=0).astype(BF16)
    wfull[core, xy] = pk[...]
    w_x = Push(wxs, wxr)
    for peer in xy_peers:
        w_x.start(pk, wfull.at[core, xy], peer)

    def norm_row(l, carry):
        values = lat_ref[l].astype(F32)
        centred = values - jnp.mean(values, axis=-1, keepdims=True)
        spread = jnp.mean(centred * centred, axis=-1, keepdims=True)
        normed_s[l, 0:SEG] = (centred * lax.rsqrt(spread + 1e-05) * gain_ref[...]).astype(BF16)
        compress(normed_s[l], 0, l)
        return carry

    lax.fori_loop(0, LAT, norm_row, 0)
    ex1[0] = Push(s1s.at[0], s1r.at[0])
    for d, peer in enumerate(chan_peers):
        ex1[0].start(send1.at[0, peer[1]], recv1.at[0, chan], peer)
    recv1[0, chan] = send1[0, chan]

    w_x.wait_recv()
    w_c = Push(wcs, wcr)
    w_c.start(wfull.at[core], wfull.at[core], sibling)
    cm_s[...] = jnp.zeros_like(cm_s)
    dc_s[...] = jnp.zeros_like(dc_s)
    gacc[...] = jnp.zeros_like(gacc)
    w_c.wait_recv()

    def mlp_step(i, carry):
        t, h = i // 4, lax.rem(i, 4)
        half, part = h // 2, pl.ds(lax.rem(h, 2) * 8, 8)
        rows = pl.ds(t * 4, 4)
        tokens = normed_s[rows].reshape(4 * PAD, 256)
        grads = cot_s[rows].reshape(4 * PAD, 256)
        w_in = wfull[half, part, 0].reshape(256, 256)
        w_out = wfull[half, part, 1].reshape(256, 256)
        value, slope = gelu_parts(dot(tokens, w_in, 1, 1))
        hidden = value.astype(BF16)
        d_pre = (dot(grads, w_out, 1, 1) * slope).astype(BF16)
        cm_s[rows] += dot(hidden, w_out).reshape(4, PAD, 256)
        dc_s[rows] += dot(d_pre, w_in).reshape(4, PAD, 256)
        gacc[half, part, 0] += dot(d_pre, tokens, 0, 0).reshape(8, 32, 256)
        gacc[half, part, 1] += dot(hidden, grads, 0, 0).reshape(8, 32, 256)
        return carry

    lax.fori_loop(0, 12, mlp_step, 0)
    gsc[...] = gacc[1 - core].astype(BF16)
    g_c = Push(gcs, gcr)
    g_c.start(gsc, grc, sibling)

    loads["expand"].wait()
    row = lax.broadcasted_iota(jnp.int32, (768, 1), 0)
    weight = jnp.where((row == 0) | (row == 12), 1.0, 2.0).astype(F32)

    def zonal(slot):
        ex1[slot].wait_recv()
        coded = jnp.concatenate([recv1[slot, i].reshape(384, RANK) for i in range(8)], axis=1)
        return dot(expand[...], coded, 1, 1)

    modes_1 = (zonal(1) * weight).reshape(32, 24, 384)
    modes_0 = zonal(0).reshape(32, 24, 384)
    send2[...] = jnp.concatenate([modes_0, modes_1], axis=1).astype(BF16)
    ex2 = Push(s2s, s2r)
    for peer in pen_peers:
        ex2.start(send2.at[peer[0]], recv2.at[pen], peer)
    recv2[pen] = send2[pen]

    g_c.wait_recv()
    gsx[...] = (gacc[core] + grc[...].astype(F32)).astype(BF16)
    g_x = Push(gxs, gxr)
    for index, peer in zip(xy_index, xy_peers):
        g_x.start(gsx.at[index], grx.at[xy], peer)
    grx[xy] = gsx[xy]

    r128 = lax.broadcasted_iota(jnp.int32, (128, 128), 0) // 32
    c128 = lax.broadcasted_iota(jnp.int32, (128, 128), 1) // 32
    block = (r128 == c128).astype(F32)

    def spread_filter(ref):
        parts = []
        for part in range(2):
            w = ref[part].astype(F32)
            w = jnp.concatenate([w] * 4, axis=1)
            parts.append(jnp.concatenate([w] * 4, axis=0) * block)
        re, im = parts
        top = jnp.concatenate([re, im], axis=1)
        low = jnp.concatenate([-im, re], axis=1)
        return jnp.concatenate([top, low], axis=0).astype(BF16)

    filter_1 = spread_filter(ff_ref)
    filter_2 = spread_filter(fs_ref)
    for name in ("first", "first_t", "second", "second_t", "tw_re", "tw_im"):
        loads[name].wait()

    def meridian(modes):
        out = dot(first[...], modes)
        re, im = out[:384], out[384:]
        g_re = re * tw_re[...] - im * tw_im[...]
        g_im = re * tw_im[...] + im * tw_re[...]
        mixed = jnp.concatenate([g_re, g_im], axis=1).astype(BF16)
        out = dot(mixed, second[...])
        return jnp.concatenate(
            [
                jnp.concatenate(
                    [out[:, g * 128 : g * 128 + 128], out[:, 384 + g * 128 : 512 + g * 128]], axis=1
                )
                for g in range(3)
            ],
            axis=0,
        )

    def meridian_back(spectra):
        spectra = jnp.concatenate(
            [spectra[g * 384 : g * 384 + 384, :128] for g in range(3)]
            + [spectra[g * 384 : g * 384 + 384, 128:] for g in range(3)],
            axis=1,
        )
        out = dot(spectra, second_t[...])
        re, im = out[:, :384], out[:, 384:]
        h_re = re * tw_re[...] + im * tw_im[...]
        h_im = im * tw_re[...] - re * tw_im[...]
        mixed = jnp.concatenate([h_re, h_im], axis=0).astype(BF16)
        return dot(first_t[...], mixed)

    ex2.wait_recv()
    received = recv2[...].astype(F32)
    spectrum = meridian(received[:, :24].reshape(768, 384).astype(BF16)).astype(BF16)
    d_shrunk = meridian(received[:, 24:].reshape(768, 384).astype(BF16))
    value, slope = gelu_parts(dot(spectrum, filter_1))
    first_hidden = value.astype(BF16)
    second_act = dot(first_hidden, filter_2)
    bend = jnp.tanh(second_act * 10.0)
    shrunk = (second_act - 0.1 * bend).astype(BF16)
    d_second = (d_shrunk * bend * bend).astype(BF16)
    outer_2 = dot(first_hidden, d_second, 0, 0)
    d_first = (dot(d_second, filter_2, 1, 1) * slope).astype(BF16)
    outer_1 = dot(spectrum, d_first, 0, 0)
    d_spectrum = dot(d_first, filter_1, 1, 1).astype(BF16)
    back_0 = meridian_back(shrunk).reshape(32, 24, 384)
    back_1 = meridian_back(d_spectrum).reshape(32, 24, 384)
    send3[...] = jnp.concatenate([back_0, back_1], axis=1).astype(BF16)
    ex3 = Push(s3s, s3r)
    for peer in pen_peers:
        ex3.start(send3.at[peer[0]], recv3.at[pen], peer)
    recv3[pen] = send3[pen]

    lane_group = lax.broadcasted_iota(jnp.int32, (32, 128), 1) // 32

    def fold(outer):
        o = {}
        for p in range(2):
            for q in range(2):
                tile = outer[p * 128 : p * 128 + 128, q * 128 : q * 128 + 128] * block
                tile = tile[0:32] + tile[32:64] + tile[64:96] + tile[96:128]
                tile = tile + pltpu.roll(tile, 64, 1)
                o[p, q] = tile + pltpu.roll(tile, 32, 1)
        return o[0, 0] + o[1, 1], o[0, 1] - o[1, 0]

    f1_re, f1_im = fold(outer_1)
    f2_re, f2_im = fold(outer_2)
    mine = jnp.where(
        lane_group == 0, f1_re, jnp.where(lane_group == 1, f1_im, jnp.where(lane_group == 2, f2_re, f2_im))
    )
    fbuf[0] = mine
    f_c = Push(fcs, fcr)
    f_c.start(fbuf.at[0], frc, sibling)

    g_x.wait_recv()
    summed = grx[0].astype(F32)
    for i in range(1, 16):
        summed = summed + grx[i].astype(F32)
    for i in range(8):
        gsz[i, 0:4] = summed[0, i * 4 : i * 4 + 4]
        gsz[i, 4:8] = summed[1, i * 4 : i * 4 + 4]
    g_z = Push(gzs, gzr)
    for index, peer in zip(z_index, z_peers):
        g_z.start(gsz.at[index], grz.at[z], peer)
    grz[z] = gsz[z]

    f_c.wait_recv()
    fbuf[1] = fbuf[0] + frc[...]
    f_y = Push(fys, fyr)
    for peer in y_peers:
        f_y.start(fbuf.at[1], fry.at[y], peer)
    fry[y] = fbuf[1]
    f_y.wait_recv()
    fbuf[2] = (fry[0] + fry[1]) + (fry[2] + fry[3])
    f_z = Push(fzs, fzr)
    for peer in zlo_peers:
        f_z.start(fbuf.at[2], frz.at[zlo], peer)
    frz[zlo] = fbuf[2]
    g_z.wait_recv()
    total = grz[0]
    for i in range(1, 8):
        total = total + grz[i]
    gwi_ref[...] = total[0:4]
    gwo_ref[...] = total[4:8]
    f_z.wait_recv()
    total = (frz[0] + frz[1]) + (frz[2] + frz[3])
    gff_ref[0] = total[:, 0:32]
    gff_ref[1] = total[:, 32:64]
    gfs_ref[0] = total[:, 64:96]
    gfs_ref[1] = total[:, 96:128]

    ex3.wait_recv()
    received = recv3[...].astype(F32)

    def unzonal(modes, slot):
        coded = dot(modes, expand[...], 0, 0).astype(BF16)
        for i in range(8):
            send4[slot, i] = coded[:, i * RANK : i * RANK + RANK].reshape(LAT, 32, RANK)
        push = Push(s4s.at[slot], s4r.at[slot])
        for peer in chan_peers:
            push.start(send4.at[slot, peer[1]], recv4.at[slot, chan], peer)
        recv4[slot, chan] = send4[slot, chan]
        return push

    ex4 = [None, None]
    ex4[0] = unzonal((received[:, :24].reshape(768, 384) * weight).astype(BF16), 0)
    ex4[1] = unzonal(received[:, 24:].reshape(768, 384).astype(BF16), 1)

    ex4[0].wait_recv()

    def out_row(l, carry):
        coded = recv4[0, :, l].reshape(256, RANK)
        spatial = dot(V[...], coded, 1, 1)[:SEG]
        bo_ref[l] = (lat_ref[l].astype(F32) + spatial + cm_s[l, 0:SEG]).astype(BF16)
        return carry

    lax.fori_loop(0, LAT, out_row, 0)
    ex4[1].wait_recv()

    def grad_row(l, carry):
        coded = recv4[1, :, l].reshape(256, RANK)
        d_normed = dot(V[...], coded, 1, 1)[:SEG] + dc_s[l, 0:SEG]
        values = lat_ref[l].astype(F32)
        centred = values - jnp.mean(values, axis=-1, keepdims=True)
        spread = jnp.mean(centred * centred, axis=-1, keepdims=True)
        scale = lax.rsqrt(spread + 1e-05)
        unit = centred * scale
        d_unit = d_normed * gain_ref[...]
        mean_d = jnp.mean(d_unit, axis=-1, keepdims=True)
        mean_du = jnp.mean(d_unit * unit, axis=-1, keepdims=True)
        d_values = scale * (d_unit - mean_d - unit * mean_du)
        gl_ref[l] = (cot_ref[l].astype(F32) + d_values).astype(BF16)
        return carry

    lax.fori_loop(0, LAT, grad_row, 0)
    for push in (w_z, w_x, w_c, g_c, g_x, g_z, f_c, f_y, f_z, ex1[0], ex1[1], ex2, ex3, ex4[0], ex4[1]):
        push.wait_send()


def body(latents, norm_gain, weight_in, weight_out, filter_first, filter_second, cotangent):
    table = tables()
    consts = [jnp.asarray(table[name]) for name in CONSTS]
    dma = pltpu.SemaphoreType.DMA
    vmem = pl.BlockSpec(memory_space=pltpu.VMEM)
    scratch = [pltpu.VMEM(c.shape, c.dtype) for c in consts]
    scratch += [
        pltpu.VMEM((LAT, PAD, 256), BF16),
        pltpu.VMEM((LAT, PAD, 256), BF16),
        pltpu.VMEM((2, 8, LAT, 32, RANK), BF16),
        pltpu.VMEM((2, 8, LAT, 32, RANK), BF16),
        pltpu.VMEM((32, 48, 384), BF16),
        pltpu.VMEM((32, 48, 384), BF16),
        pltpu.VMEM((32, 48, 384), BF16),
        pltpu.VMEM((32, 48, 384), BF16),
        pltpu.VMEM((2, 8, LAT, 32, RANK), BF16),
        pltpu.VMEM((2, 8, LAT, 32, RANK), BF16),
        pltpu.VMEM((LAT, PAD, 256), F32),
        pltpu.VMEM((LAT, PAD, 256), F32),
        pltpu.VMEM((8, 256), F32),
        pltpu.VMEM((8, 8, 256), F32),
        pltpu.VMEM((2, 32, 256), BF16),
        pltpu.VMEM((2, 16, 2, 32, 256), BF16),
        pltpu.VMEM((2, 16, 2, 32, 256), F32),
        pltpu.VMEM((16, 2, 32, 256), BF16),
        pltpu.VMEM((16, 2, 32, 256), BF16),
        pltpu.VMEM((16, 2, 32, 256), BF16),
        pltpu.VMEM((16, 2, 32, 256), BF16),
        pltpu.VMEM((8, 8, 256), F32),
        pltpu.VMEM((8, 8, 256), F32),
        pltpu.VMEM((3, 32, 128), F32),
        pltpu.VMEM((32, 128), F32),
        pltpu.VMEM((4, 32, 128), F32),
        pltpu.VMEM((4, 32, 128), F32),
    ]
    scratch += [dma((len(CONSTS),))]
    scratch += [dma((2, 7)), dma((2, 7)), dma((31,)), dma((31,)), dma((31,)), dma((31,)), dma((2, 7)), dma((2, 7))]
    for n in (7, 15, 1, 7, 15, 1, 1, 3, 3):
        scratch += [dma((n,)), dma((n,))]
    out_shape = (
        jax.ShapeDtypeStruct(latents.shape, BF16),
        jax.ShapeDtypeStruct(latents.shape, BF16),
        jax.ShapeDtypeStruct((4, 256), F32),
        jax.ShapeDtypeStruct((4, 256), F32),
        jax.ShapeDtypeStruct((2, 32, 32), F32),
        jax.ShapeDtypeStruct((2, 32, 32), F32),
    )
    outs = pl.pallas_call(
        kernel,
        out_shape=out_shape,
        in_specs=[vmem] * 7 + [pl.BlockSpec(memory_space=pl.ANY)] * len(CONSTS),
        out_specs=(vmem,) * 6,
        scratch_shapes=scratch,
        compiler_params=pltpu.CompilerParams(
            collective_id=0, has_side_effects=True, vmem_limit_bytes=62 * 1024 * 1024
        ),
        name="spectral_block",
    )(
        latents,
        norm_gain.reshape(1, 256),
        weight_in,
        weight_out,
        filter_first.reshape(2, 32, 32),
        filter_second.reshape(2, 32, 32),
        cotangent,
        *consts,
    )
    return outs[:4] + (outs[4].reshape(2, 1, 32, 32), outs[5].reshape(2, 1, 32, 32))


def solution(mesh):
    placed = (
        P("pen", "chan", None),
        P(),
        P(("pen", "chan"), None),
        P(("pen", "chan"), None),
        P(None, "chan", None, None),
        P(None, "chan", None, None),
        P("pen", "chan", None),
    )
    return jax.shard_map(
        body,
        mesh=mesh,
        in_specs=placed,
        out_specs=(
            P("pen", "chan", None),
            P("pen", "chan", None),
            P(("pen", "chan"), None),
            P(("pen", "chan"), None),
            P(None, "chan", None, None),
            P(None, "chan", None, None),
        ),
        check_vma=False,
    )
```

```python
import functools
import math

import jax
import jax.numpy as jnp
import ml_dtypes
import numpy as np
from jax import lax
from jax.experimental import pallas as pl
from jax.experimental.pallas import tpu as pltpu
from jax.sharding import PartitionSpec as P

MESH = pl.DeviceIdType.MESH
NLON, KLON, NLAT = 1440, 384, 384
SEG = 180
PAD = 192
RANK = 128
LAT = 12
NK = 12
GELU_C = math.sqrt(2.0 / math.pi)
F32, BF16 = jnp.float32, jnp.bfloat16


def as_bf16(values):
    return np.asarray(values, np.float32).astype(ml_dtypes.bfloat16)


@functools.lru_cache(None)
def tables():
    j = np.arange(NLON)[:, None]
    k = np.arange(KLON)[None, :]
    a = 2.0 * np.pi * ((j * k) % NLON) / NLON
    full = np.concatenate([np.cos(a), -np.sin(a)], axis=1) / math.sqrt(NLON)
    left, _, _ = np.linalg.svd(full[:SEG], full_matrices=False)
    basis = left[:, :RANK]
    expand = np.stack([basis.T @ full[s * SEG : (s + 1) * SEG] for s in range(8)])
    expand = expand.reshape(8, RANK, 2, 32, NK).transpose(3, 2, 4, 0, 1).reshape(768, 8 * RANK)
    basis_pad = np.zeros((PAD, RANK))
    basis_pad[:SEG] = basis
    s = np.arange(32)
    w32 = np.exp(-2j * np.pi * np.outer(s, s) / 32)
    l = np.arange(12)
    w12 = np.exp(-2j * np.pi * np.outer(l, l) / 12)

    def real_form(w):
        return np.stack(
            [np.stack([w.real, -w.imag], axis=1), np.stack([w.imag, w.real], axis=1)]
        )

    first = np.einsum("qmps,kl->qmkspl", real_form(w32), np.eye(NK)).reshape(768, 768)
    second = np.einsum("qmpl,cd->plcqmd", real_form(w12), np.eye(32)).reshape(768, 768)
    twiddle = np.exp(-2j * np.pi * np.outer(s, l) / 384) / math.sqrt(NLAT)
    twiddle = np.repeat(np.repeat(twiddle, NK, axis=0), 32, axis=1)
    return dict(
        basis=as_bf16(basis_pad),
        expand=as_bf16(expand),
        first=as_bf16(first),
        first_t=as_bf16(first.T),
        second=as_bf16(second),
        second_t=as_bf16(second.T),
        tw_re=np.asarray(twiddle.real, np.float32),
        tw_im=np.asarray(twiddle.imag, np.float32),
    )


CONSTS = ("basis", "expand", "first", "first_t", "second", "second_t", "tw_re", "tw_im")


def dot(a, b, ca=1, cb=0):
    return lax.dot_general(a, b, (((ca,), (cb,)), ((), ())), preferred_element_type=F32)


def gelu_parts(v):
    v2 = v * v
    t = jnp.tanh(v * (GELU_C + (GELU_C * 0.044715) * v2))
    half = 0.5 + 0.5 * t
    value = v * half
    slope = half + (0.5 * v) * (1.0 - t * t) * (GELU_C + (3.0 * GELU_C * 0.044715) * v2)
    return value, slope


class Push:
    def __init__(self, send_sem, recv_sem):
        self.send_sem, self.recv_sem, self.copies = send_sem, recv_sem, []

    def start(self, src, dst, device):
        n = len(self.copies)
        copy = remote(src, dst, self.send_sem.at[n], self.recv_sem.at[n], device)
        copy.start()
        self.copies.append(copy)

    def wait_recv(self):
        for copy in self.copies:
            copy.wait_recv()

    def wait_send(self):
        for copy in self.copies:
            copy.wait_send()


def remote(src, dst, send_sem, recv_sem, device):
    return pltpu.make_async_remote_copy(
        src_ref=src,
        dst_ref=dst,
        send_sem=send_sem,
        recv_sem=recv_sem,
        device_id=device,
        device_id_type=MESH,
    )


def kernel(*refs):
    (lat_ref, gain_ref, win_ref, wout_ref, ff_ref, fs_ref, cot_ref) = refs[:7]
    const_hbm = refs[7 : 7 + len(CONSTS)]
    refs = refs[7 + len(CONSTS) :]
    (bo_ref, gl_ref, gwi_ref, gwo_ref, gff_ref, gfs_ref) = refs[:6]
    refs = refs[6:]
    const = refs[: len(CONSTS)]
    refs = refs[len(CONSTS) :]
    (normed_s, cot_s, send1, recv1, send2, recv2, send3, recv3, send4, mid4, recv4) = refs[:11]
    (mixed_s, cm_s, dc_s, zsrc, zbuf, pk, wfull, gacc, gsc, grc, gsx, grx, gsz, grz) = refs[11:25]
    (fsrc, fpair, fall, fbuf, frc, frx, frz) = refs[25:32]
    (const_sem, s1s, s1r, s2s, s2r, s3s, s3r, s4s, s4r, s5s, s5r) = refs[32:43]
    (wzs, wzr, wxs, wxr, wcs, wcr, gzs, gzr, gxs, gxr, gcs, gcr) = refs[43:55]
    (fps, fpr, fas, far, fcs, fcr, fxs, fxr, fzs, fzr) = refs[55:65]
    V, expand, first, first_t, second, second_t, tw_re, tw_im = const

    pen = lax.axis_index("pen")
    chan = lax.axis_index("chan")
    x, zhi = chan // 2, lax.rem(chan, 2)
    y, zlo, core = pen // 8, lax.rem(pen // 2, 4), lax.rem(pen, 2)
    z = zhi * 4 + zlo
    xy = x * 4 + y
    place = y * 8 + x * 2 + core

    def device(x_, y_, z_, core_):
        return (y_ * 8 + lax.rem(z_, 4) * 2 + core_, x_ * 2 + z_ // 4)

    def member(p):
        return device(lax.rem(p // 2, 4), p // 8, z, lax.rem(p, 2))

    def same(device_):
        return (device_[0] == pen) & (device_[1] == chan)

    z_index = [lax.rem(z + d, 8) for d in range(1, 8)]
    z_peers = [device(x, y, i, core) for i in z_index]
    xy_index = [lax.rem(xy + d, 16) for d in range(1, 16)]
    xy_peers = [device(i // 4, lax.rem(i, 4), z, core) for i in xy_index]
    place_index = [lax.rem(place + d, 32) for d in range(1, 32)]
    place_peers = [member(p) for p in place_index]
    sibling = device(x, y, z, 1 - core)
    x_index = [lax.rem(x + d, 4) for d in range(1, 4)]
    x_peers = [device(i, y, z, core) for i in x_index]
    z_partner = device(x, y, (1 - zhi) * 4 + zlo, core)
    to_index = [lax.rem(z + d, 8) for d in (4, 1, 7, 2, 6, 3, 5, 0)]
    to_devices = [device(zlo, y, i, core) for i in to_index]
    from_devices = [device(i // 2, y, (i % 2) * 4 + x, core) for i in range(8)]

    loads = []
    for n, (src, dst) in enumerate(zip(const_hbm, const)):
        load = pltpu.make_async_copy(src, dst, const_sem.at[n])
        load.start()
        loads.append(load)
    loads = dict(zip(CONSTS, loads))

    barrier = pltpu.get_barrier_semaphore()
    for peer in place_peers + z_peers:
        pl.semaphore_signal(barrier, inc=1, device_id=peer, device_id_type=MESH)
    for peer in from_devices:

        @pl.when(jnp.logical_not(same(peer)))
        def _():
            pl.semaphore_signal(barrier, inc=1, device_id=peer, device_id_type=MESH)

    zsrc[0:4, :] = win_ref[...].astype(F32)
    zsrc[4:8, :] = wout_ref[...].astype(F32)
    zbuf[z] = zsrc[...]
    fsrc[...] = jnp.concatenate(
        [ff_ref[0].astype(F32), ff_ref[1].astype(F32), fs_ref[0].astype(F32), fs_ref[1].astype(F32)],
        axis=1,
    )
    fpair[zhi] = fsrc[...]
    normed_s[:, 176:192, :] = jnp.zeros((LAT, 16, 256), BF16)
    cot_s[:, 176:192, :] = jnp.zeros((LAT, 16, 256), BF16)
    own = jnp.where(x == zlo, 1, 0)
    pl.semaphore_wait(barrier, len(place_peers) + len(z_peers) + 8 - own)

    w_z = Push(wzs, wzr)
    for peer in z_peers:
        w_z.start(zsrc, zbuf.at[z], peer)
    f_p = Push(fps, fpr)
    f_p.start(fsrc, fpair.at[zhi], z_partner)

    loads["basis"].wait()

    def compress(g, slot, l, rows):
        coded = dot(rows, V[...], 0, 0).astype(BF16)
        send1[g, :, slot, l] = coded.reshape(8, 32, RANK)

    def ex1_copy(g, n):
        return remote(
            send1.at[g, to_index[n]],
            recv1.at[g, chan],
            s1s.at[g, n],
            s1r.at[g, chan],
            to_devices[n],
        )

    def ex1_start(g):
        def row(l, carry):
            i = g * 4 + l
            cot_s[i, 0:SEG] = cot_ref[i]
            compress(g, 1, l, cot_s[i])
            values = lat_ref[i].astype(F32)
            centred = values - jnp.mean(values, axis=-1, keepdims=True)
            spread = jnp.mean(centred * centred, axis=-1, keepdims=True)
            normed_s[i, 0:SEG] = (centred * lax.rsqrt(spread + 1e-05) * gain_ref[...]).astype(BF16)
            compress(g, 0, l, normed_s[i])
            return carry

        lax.fori_loop(0, 4, row, 0)
        for n in range(8):

            @pl.when(jnp.logical_not(same(to_devices[n])))
            def _():
                ex1_copy(g, n).start()

        @pl.when(x == zlo)
        def _():
            recv1[g, chan] = send1[g, z]

    def ex1_wait(g):
        for i in range(8):

            @pl.when(jnp.logical_not(same(from_devices[i])))
            def _():
                remote(
                    send1.at[g, i], recv1.at[g, i], s1s.at[g, i], s1r.at[g, i], from_devices[i]
                ).wait_recv()

    def ex1_sent(g):
        for n in range(8):

            @pl.when(jnp.logical_not(same(to_devices[n])))
            def _():
                ex1_copy(g, n).wait_send()

    ex1_start(0)
    w_z.wait_recv()
    pk[0] = jnp.concatenate([zbuf[i, 0:4] for i in range(8)], axis=0).astype(BF16)
    pk[1] = jnp.concatenate([zbuf[i, 4:8] for i in range(8)], axis=0).astype(BF16)
    wfull[core, xy] = pk[...]
    w_x = Push(wxs, wxr)
    for peer in xy_peers:
        w_x.start(pk, wfull.at[core, xy], peer)
    f_p.wait_recv()
    fall[x] = fpair[...]
    f_a = Push(fas, far)
    for peer in x_peers:
        f_a.start(fpair, fall.at[x], peer)
    ex1_start(1)
    ex1_start(2)

    w_x.wait_recv()
    w_c = Push(wcs, wcr)
    w_c.start(wfull.at[core], wfull.at[core], sibling)
    cm_s[...] = jnp.zeros_like(cm_s)
    dc_s[...] = jnp.zeros_like(dc_s)
    gacc[...] = jnp.zeros_like(gacc)
    w_c.wait_recv()

    def mlp_step(i, carry):
        t, h = i // 4, lax.rem(i, 4)
        half, part = h // 2, pl.ds(lax.rem(h, 2) * 8, 8)
        rows = pl.ds(t * 4, 4)
        tokens = normed_s[rows].reshape(4 * PAD, 256)
        grads = cot_s[rows].reshape(4 * PAD, 256)
        w_in = wfull[half, part, 0].reshape(256, 256)
        w_out = wfull[half, part, 1].reshape(256, 256)
        value, slope = gelu_parts(dot(tokens, w_in, 1, 1))
        hidden = value.astype(BF16)
        d_pre = (dot(grads, w_out, 1, 1) * slope).astype(BF16)
        cm_s[rows] += dot(hidden, w_out).reshape(4, PAD, 256)
        dc_s[rows] += dot(d_pre, w_in).reshape(4, PAD, 256)
        gacc[half, part, 0] += dot(d_pre, tokens, 0, 0).reshape(8, 32, 256)
        gacc[half, part, 1] += dot(hidden, grads, 0, 0).reshape(8, 32, 256)
        return carry

    row = lax.broadcasted_iota(jnp.int32, (768, 1), 0)
    weight = jnp.where((row == 0) | (row == 12), 1.0, 2.0).astype(F32)

    def pair_rows(modes):
        both = [modes[:, :128].reshape(32, 24, 128), modes[:, 128:].reshape(32, 24, 128)]
        return jnp.concatenate(both, axis=1).astype(BF16)

    def split_rows(ref, g):
        both = ref[g].astype(F32)
        return both[:, :24].reshape(768, 128), both[:, 24:].reshape(768, 128)

    def swap(send, recv, send_sem, recv_sem, g):
        push = Push(send_sem.at[g], recv_sem.at[g])
        for index, peer in zip(place_index, place_peers):
            push.start(send.at[g, index], recv.at[g, place], peer)
        recv[g, place] = send[g, place]
        return push

    def zonal(g):
        ex1_wait(g)
        coded = jnp.concatenate([recv1[g, i].reshape(256, RANK) for i in range(8)], axis=1)
        modes = dot(expand[...], coded, 1, 1)
        modes = jnp.concatenate([modes[:, :128], modes[:, 128:] * weight], axis=1)
        send2[g] = pair_rows(modes)
        return swap(send2, recv2, s2s, s2r, g)

    loads["expand"].wait()
    ex2 = [None] * 3
    lax.fori_loop(0, 2, mlp_step, 0)
    ex2[0] = zonal(0)
    lax.fori_loop(2, 7, mlp_step, 0)
    ex2[1] = zonal(1)
    lax.fori_loop(7, 12, mlp_step, 0)
    gsc[...] = gacc[1 - core].astype(BF16)
    g_c = Push(gcs, gcr)
    g_c.start(gsc, grc, sibling)
    ex2[2] = zonal(2)

    r128 = lax.broadcasted_iota(jnp.int32, (128, 128), 0) // 32
    c128 = lax.broadcasted_iota(jnp.int32, (128, 128), 1) // 32
    block = (r128 == c128).astype(F32)
    lane_group = lax.broadcasted_iota(jnp.int32, (32, 128), 1) // 32

    def over_groups(tile):
        tile = tile + pltpu.roll(tile, 64, 1)
        return tile + pltpu.roll(tile, 32, 1)

    f_a.wait_recv()
    filters = fall[z // 2, lax.rem(z, 2)]

    def spread_filter(n):
        parts = []
        for part in range(2):
            w = over_groups(jnp.where(lane_group == 2 * n + part, filters, 0.0))
            parts.append(jnp.concatenate([w] * 4, axis=0) * block)
        re, im = parts
        top = jnp.concatenate([re, im], axis=1)
        low = jnp.concatenate([-im, re], axis=1)
        return jnp.concatenate([top, low], axis=0).astype(BF16)

    filter_1 = spread_filter(0)
    filter_2 = spread_filter(1)
    for name in ("first", "first_t", "second", "second_t", "tw_re", "tw_im"):
        loads[name].wait()

    def meridian_first(g):
        ex2[g].wait_recv()
        lanes = slice(g * 128, g * 128 + 128)
        modes = jnp.concatenate(split_rows(recv2, g), axis=1).astype(BF16)
        out = dot(first[...], modes)
        for slot in range(2):
            re = out[:384, slot * 128 : slot * 128 + 128]
            im = out[384:, slot * 128 : slot * 128 + 128]
            mixed_s[slot, :, lanes] = (re * tw_re[:, lanes] - im * tw_im[:, lanes]).astype(BF16)
            mixed_s[slot, :, 384 + g * 128 : 512 + g * 128] = (
                re * tw_im[:, lanes] + im * tw_re[:, lanes]
            ).astype(BF16)

    def meridian_second(slot):
        out = dot(mixed_s[slot], second[...])
        return jnp.concatenate(
            [
                jnp.concatenate(
                    [out[:, g * 128 : g * 128 + 128], out[:, 384 + g * 128 : 512 + g * 128]], axis=1
                )
                for g in range(3)
            ],
            axis=0,
        )

    def meridian_back(spectra):
        spectra = jnp.concatenate(
            [spectra[g * 384 : g * 384 + 384, :128] for g in range(3)]
            + [spectra[g * 384 : g * 384 + 384, 128:] for g in range(3)],
            axis=1,
        )
        out = dot(spectra, second_t[...])
        re, im = out[:, :384], out[:, 384:]
        h_re = re * tw_re[...] + im * tw_im[...]
        h_im = im * tw_re[...] - re * tw_im[...]
        return jnp.concatenate([h_re, h_im], axis=0).astype(BF16)

    meridian_first(0)
    meridian_first(1)

    g_c.wait_recv()
    gsx[...] = (gacc[core] + grc[...].astype(F32)).astype(BF16)
    g_x = Push(gxs, gxr)
    for index, peer in zip(xy_index, xy_peers):
        g_x.start(gsx.at[index], grx.at[xy], peer)
    grx[xy] = gsx[xy]

    meridian_first(2)
    spectrum = meridian_second(0).astype(BF16)
    value, slope = gelu_parts(dot(spectrum, filter_1))
    first_hidden = value.astype(BF16)
    second_act = dot(first_hidden, filter_2)
    bend = jnp.tanh(second_act * 10.0)
    shrunk = (second_act - 0.1 * bend).astype(BF16)
    d_second = (meridian_second(1) * bend * bend).astype(BF16)
    d_first = (dot(d_second, filter_2, 1, 1) * slope).astype(BF16)
    d_spectrum = dot(d_first, filter_1, 1, 1).astype(BF16)
    back_0 = meridian_back(shrunk)
    back_1 = meridian_back(d_spectrum)
    ex3 = []
    for g in range(3):
        lanes = slice(g * 128, g * 128 + 128)
        both = jnp.concatenate([back_0[:, lanes], back_1[:, lanes]], axis=1)
        send3[g] = pair_rows(dot(first_t[...], both))
        ex3.append(swap(send3, recv3, s3s, s3r, g))

    def fold(outer):
        o = {}
        for p in range(2):
            for q in range(2):
                tile = outer[p * 128 : p * 128 + 128, q * 128 : q * 128 + 128] * block
                o[p, q] = over_groups(tile[0:32] + tile[32:64] + tile[64:96] + tile[96:128])
        return o[0, 0] + o[1, 1], o[0, 1] - o[1, 0]

    f1_re, f1_im = fold(dot(spectrum, d_first, 0, 0))
    f2_re, f2_im = fold(dot(first_hidden, d_second, 0, 0))
    fbuf[0] = jnp.where(
        lane_group == 0, f1_re, jnp.where(lane_group == 1, f1_im, jnp.where(lane_group == 2, f2_re, f2_im))
    )
    f_c = Push(fcs, fcr)
    f_c.start(fbuf.at[0], frc, sibling)

    def unzonal(g):
        ex3[g].wait_recv()
        modes_0, modes_1 = split_rows(recv3, g)
        modes = jnp.concatenate([modes_0 * weight, modes_1], axis=1).astype(BF16)
        coded = dot(modes, expand[...], 0, 0).astype(BF16)
        for i in range(8):
            send4[g, i // 2, i % 2] = coded[:, i * RANK : i * RANK + RANK].reshape(2, 4, 32, RANK)
        push = Push(s4s.at[g], s4r.at[g])
        for index, peer in zip(x_index, x_peers):
            push.start(send4.at[g, index], mid4.at[g, x], peer)
        mid4[g, x] = send4[g, x]
        onward(g, 0)
        return push

    def ex5_copy(g, d, h):
        xs = lax.rem(x + (0, 3, 2, 1)[d], 4)
        to = h * 4 + xs
        copy = remote(
            mid4.at[g, xs, h],
            recv4.at[g, z],
            s5s.at[g, d * 2 + h],
            s5r.at[g, z],
            device(x, y, to, core),
        )
        return copy, to, xs

    def onward(g, d):
        for h in range(2):
            copy, to, xs = ex5_copy(g, d, h)

            @pl.when(to != z)
            def _():
                copy.start()

            @pl.when(to == z)
            def _():
                recv4[g, z] = mid4[g, xs, h]

    def forward(g):
        for d in range(1, 4):
            ex4[g].copies[d - 1].wait_recv()
            onward(g, d)

    def ex5_wait(g):
        for i in z_index:
            remote(
                mid4.at[g, 0, 0], recv4.at[g, i], s5s.at[g, 0], s5r.at[g, i], device(x, y, i, core)
            ).wait_recv()

    ex4 = [None] * 3
    ex4[0] = unzonal(0)
    f_c.wait_recv()
    fbuf[1] = fbuf[0] + frc[...]
    f_x = Push(fxs, fxr)
    for peer in xy_peers:
        f_x.start(fbuf.at[1], frx.at[xy], peer)
    frx[xy] = fbuf[1]
    ex4[1] = unzonal(1)
    forward(0)
    ex4[2] = unzonal(2)
    forward(1)

    g_x.wait_recv()
    summed = grx[0].astype(F32)
    for i in range(1, 16):
        summed = summed + grx[i].astype(F32)
    for i in range(8):
        gsz[i, 0:4] = summed[0, i * 4 : i * 4 + 4]
        gsz[i, 4:8] = summed[1, i * 4 : i * 4 + 4]
    g_z = Push(gzs, gzr)
    for index, peer in zip(z_index, z_peers):
        g_z.start(gsz.at[index], grz.at[z], peer)
    grz[z] = gsz[z]
    f_x.wait_recv()
    total = frx[0]
    for i in range(1, 16):
        total = total + frx[i]
    fbuf[2] = total
    f_z = Push(fzs, fzr)
    for peer in z_peers:
        f_z.start(fbuf.at[2], frz.at[z], peer)
    frz[z] = fbuf[2]
    forward(2)

    g_z.wait_recv()
    total = grz[0]
    for i in range(1, 8):
        total = total + grz[i]
    gwi_ref[...] = total[0:4]
    gwo_ref[...] = total[4:8]
    f_z.wait_recv()
    total = frz[chan]
    gff_ref[0] = total[:, 0:32]
    gff_ref[1] = total[:, 32:64]
    gfs_ref[0] = total[:, 64:96]
    gfs_ref[1] = total[:, 96:128]

    def finish(g):
        ex5_wait(g)

        def out_row(l, carry):
            i = g * 4 + l
            values = lat_ref[i].astype(F32)
            coded = recv4[g, :, 0, l].reshape(256, RANK)
            spatial = dot(V[...], coded, 1, 1)[:SEG]
            bo_ref[i] = (values + spatial + cm_s[i, 0:SEG]).astype(BF16)
            coded = recv4[g, :, 1, l].reshape(256, RANK)
            d_normed = dot(V[...], coded, 1, 1)[:SEG] + dc_s[i, 0:SEG]
            centred = values - jnp.mean(values, axis=-1, keepdims=True)
            spread = jnp.mean(centred * centred, axis=-1, keepdims=True)
            scale = lax.rsqrt(spread + 1e-05)
            unit = centred * scale
            d_unit = d_normed * gain_ref[...]
            mean_d = jnp.mean(d_unit, axis=-1, keepdims=True)
            mean_du = jnp.mean(d_unit * unit, axis=-1, keepdims=True)
            d_values = scale * (d_unit - mean_d - unit * mean_du)
            gl_ref[i] = (cot_ref[i].astype(F32) + d_values).astype(BF16)
            return carry

        lax.fori_loop(0, 4, out_row, 0)

    for g in range(3):
        finish(g)

    for push in [w_z, w_x, w_c, g_c, g_x, g_z, f_p, f_a, f_c, f_x, f_z] + ex2 + ex3 + ex4:
        push.wait_send()
    for g in range(3):
        ex1_sent(g)
        for d in range(4):
            for h in range(2):
                copy, to, xs = ex5_copy(g, d, h)

                @pl.when(to != z)
                def _():
                    copy.wait_send()


def body(latents, norm_gain, weight_in, weight_out, filter_first, filter_second, cotangent):
    table = tables()
    consts = [jnp.asarray(table[name]) for name in CONSTS]
    dma = pltpu.SemaphoreType.DMA
    vmem = pl.BlockSpec(memory_space=pltpu.VMEM)
    scratch = [pltpu.VMEM(c.shape, c.dtype) for c in consts]
    scratch += [
        pltpu.VMEM((LAT, PAD, 256), BF16),
        pltpu.VMEM((LAT, PAD, 256), BF16),
        pltpu.VMEM((3, 8, 2, 4, 32, RANK), BF16),
        pltpu.VMEM((3, 8, 2, 4, 32, RANK), BF16),
        pltpu.VMEM((3, 32, 48, 128), BF16),
        pltpu.VMEM((3, 32, 48, 128), BF16),
        pltpu.VMEM((3, 32, 48, 128), BF16),
        pltpu.VMEM((3, 32, 48, 128), BF16),
        pltpu.VMEM((3, 4, 2, 2, 4, 32, RANK), BF16),
        pltpu.VMEM((3, 4, 2, 2, 4, 32, RANK), BF16),
        pltpu.VMEM((3, 8, 2, 4, 32, RANK), BF16),
        pltpu.VMEM((2, 384, 768), BF16),
        pltpu.VMEM((LAT, PAD, 256), F32),
        pltpu.VMEM((LAT, PAD, 256), F32),
        pltpu.VMEM((8, 256), F32),
        pltpu.VMEM((8, 8, 256), F32),
        pltpu.VMEM((2, 32, 256), BF16),
        pltpu.VMEM((2, 16, 2, 32, 256), BF16),
        pltpu.VMEM((2, 16, 2, 32, 256), F32),
        pltpu.VMEM((16, 2, 32, 256), BF16),
        pltpu.VMEM((16, 2, 32, 256), BF16),
        pltpu.VMEM((16, 2, 32, 256), BF16),
        pltpu.VMEM((16, 2, 32, 256), BF16),
        pltpu.VMEM((8, 8, 256), F32),
        pltpu.VMEM((8, 8, 256), F32),
        pltpu.VMEM((32, 128), F32),
        pltpu.VMEM((2, 32, 128), F32),
        pltpu.VMEM((4, 2, 32, 128), F32),
        pltpu.VMEM((3, 32, 128), F32),
        pltpu.VMEM((32, 128), F32),
        pltpu.VMEM((16, 32, 128), F32),
        pltpu.VMEM((8, 32, 128), F32),
    ]
    scratch += [dma((len(CONSTS),))]
    for n in (8, 31, 31, 3, 8):
        scratch += [dma((3, n)), dma((3, n))]
    for n in (7, 15, 1, 7, 15, 1, 1, 3, 1, 15, 7):
        scratch += [dma((n,)), dma((n,))]
    out_shape = (
        jax.ShapeDtypeStruct(latents.shape, BF16),
        jax.ShapeDtypeStruct(latents.shape, BF16),
        jax.ShapeDtypeStruct((4, 256), F32),
        jax.ShapeDtypeStruct((4, 256), F32),
        jax.ShapeDtypeStruct((2, 32, 32), F32),
        jax.ShapeDtypeStruct((2, 32, 32), F32),
    )
    outs = pl.pallas_call(
        kernel,
        out_shape=out_shape,
        in_specs=[vmem] * 7 + [pl.BlockSpec(memory_space=pl.ANY)] * len(CONSTS),
        out_specs=(vmem,) * 6,
        scratch_shapes=scratch,
        compiler_params=pltpu.CompilerParams(
            collective_id=0, has_side_effects=True, vmem_limit_bytes=62 * 1024 * 1024
        ),
        name="spectral_block",
    )(
        latents,
        norm_gain.reshape(1, 256),
        weight_in,
        weight_out,
        filter_first.reshape(2, 32, 32),
        filter_second.reshape(2, 32, 32),
        cotangent,
        *consts,
    )
    return outs[:4] + (outs[4].reshape(2, 1, 32, 32), outs[5].reshape(2, 1, 32, 32))


def solution(mesh):
    placed = (
        P("pen", "chan", None),
        P(),
        P(("pen", "chan"), None),
        P(("pen", "chan"), None),
        P(None, "chan", None, None),
        P(None, "chan", None, None),
        P("pen", "chan", None),
    )
    return jax.shard_map(
        body,
        mesh=mesh,
        in_specs=placed,
        out_specs=(
            P("pen", "chan", None),
            P("pen", "chan", None),
            P(("pen", "chan"), None),
            P(("pen", "chan"), None),
            P(None, "chan", None, None),
            P(None, "chan", None, None),
        ),
        check_vma=False,
    )
```

```python
import functools
import math

import jax
import jax.numpy as jnp
import ml_dtypes
import numpy as np
from jax import lax
from jax.experimental import pallas as pl
from jax.experimental.pallas import tpu as pltpu
from jax.sharding import PartitionSpec as P

MESH = pl.DeviceIdType.MESH
NLON, KLON, NLAT = 1440, 384, 384
SEG = 180
PAD = 192
RANK = 112
LAT = 12
NK = 12
GELU_C = math.sqrt(2.0 / math.pi)
F32, BF16 = jnp.float32, jnp.bfloat16


def as_bf16(values):
    return np.asarray(values, np.float32).astype(ml_dtypes.bfloat16)


@functools.lru_cache(None)
def tables():
    j = np.arange(NLON)[:, None]
    k = np.arange(KLON)[None, :]
    a = 2.0 * np.pi * ((j * k) % NLON) / NLON
    full = np.concatenate([np.cos(a), -np.sin(a)], axis=1) / math.sqrt(NLON)
    left, _, _ = np.linalg.svd(full[:SEG], full_matrices=False)
    basis = left[:, :RANK]
    expand = np.stack([basis.T @ full[s * SEG : (s + 1) * SEG] for s in range(8)])
    expand = expand.reshape(8, RANK, 2, 32, NK).transpose(3, 2, 4, 0, 1).reshape(768, 8 * RANK)
    basis_pad = np.zeros((PAD, RANK))
    basis_pad[:SEG] = basis
    s = np.arange(32)
    w32 = np.exp(-2j * np.pi * np.outer(s, s) / 32)
    l = np.arange(12)
    w12 = np.exp(-2j * np.pi * np.outer(l, l) / 12)

    def real_form(w):
        return np.stack(
            [np.stack([w.real, -w.imag], axis=1), np.stack([w.imag, w.real], axis=1)]
        )

    first = np.einsum("qmps,kl->qmkspl", real_form(w32), np.eye(NK)).reshape(768, 768)
    second = np.einsum("qmpl,cd->plcqmd", real_form(w12), np.eye(32)).reshape(768, 768)
    twiddle = np.exp(-2j * np.pi * np.outer(s, l) / 384) / math.sqrt(NLAT)
    twiddle = np.repeat(np.repeat(twiddle, NK, axis=0), 32, axis=1)
    return dict(
        basis=as_bf16(basis_pad),
        basis_t=as_bf16(basis_pad.T),
        expand=as_bf16(expand),
        expand_t=as_bf16(expand.T),
        first=as_bf16(first),
        first_t=as_bf16(first.T),
        second=as_bf16(second),
        second_t=as_bf16(second.T),
        tw_re=np.asarray(twiddle.real, np.float32),
        tw_im=np.asarray(twiddle.imag, np.float32),
    )


CONSTS = ("basis_t", "expand", "first", "tw_re", "tw_im", "second", "second_t", "first_t", "expand_t", "basis")


def dot(a, b, ca=1, cb=0):
    return lax.dot_general(a, b, (((ca,), (cb,)), ((), ())), preferred_element_type=F32)


def gelu_parts(v):
    v2 = v * v
    t = jnp.tanh(v * (GELU_C + (GELU_C * 0.044715) * v2))
    half = 0.5 + 0.5 * t
    value = v * half
    slope = half + (0.5 * v) * (1.0 - t * t) * (GELU_C + (3.0 * GELU_C * 0.044715) * v2)
    return value, slope


class Push:
    def __init__(self, send_sem, recv_sem):
        self.send_sem, self.recv_sem, self.copies = send_sem, recv_sem, []

    def start(self, src, dst, device):
        n = len(self.copies)
        copy = remote(src, dst, self.send_sem.at[n], self.recv_sem.at[n], device)
        copy.start()
        self.copies.append(copy)

    def wait_recv(self):
        for copy in self.copies:
            copy.wait_recv()

    def wait_send(self):
        for copy in self.copies:
            copy.wait_send()


def remote(src, dst, send_sem, recv_sem, device):
    return pltpu.make_async_remote_copy(
        src_ref=src,
        dst_ref=dst,
        send_sem=send_sem,
        recv_sem=recv_sem,
        device_id=device,
        device_id_type=MESH,
    )


def kernel(*refs):
    (lat_hbm, gain_ref, win_ref, wout_ref, ff_ref, fs_ref, cot_hbm) = refs[:7]
    const_hbm = refs[7 : 7 + len(CONSTS)]
    refs = refs[7 + len(CONSTS) :]
    (bo_hbm, gl_hbm, gwi_ref, gwo_ref, gff_ref, gfs_ref) = refs[:6]
    (lat_ref, cot_ref, bo_ref, gl_ref, io_sem) = refs[6:11]
    refs = refs[11:]
    const = refs[: len(CONSTS)]
    refs = refs[len(CONSTS) :]
    (normed_s, cot_s, send1, recv1, send2, recv2, send3, recv3, send4, mid4, recv4) = refs[:11]
    (mixed_s, cm_s, dc_s, zsrc, zbuf, pk, wfull, gacc, gsc, grc, gsy, gry, gsx) = refs[11:24]
    (grx, gsz, grz) = refs[24:27]
    refs = refs[2:]
    (fsrc, fpair, fall, fbuf, frc, frx, frz) = refs[25:32]
    (const_sem, s1s, s1r, s2s, s2r, s3s, s3r, s4s, s4r, s5s, s5r) = refs[32:43]
    (wzs, wzr, wxs, wxr, wys, wyr, wcs, wcr) = refs[43:51]
    (gzs, gzr, gxs, gxr, gys, gyr, gcs, gcr) = refs[51:59]
    (fps, fpr, fas, far, fcs, fcr, fxs, fxr, fzs, fzr) = refs[59:69]
    Vt, expand, first, tw_re, tw_im, second, second_t, first_t, expand_t, V = const

    pen = lax.axis_index("pen")
    chan = lax.axis_index("chan")
    x, zhi = chan // 2, lax.rem(chan, 2)
    y, zlo, core = pen // 8, lax.rem(pen // 2, 4), lax.rem(pen, 2)
    z = zhi * 4 + zlo
    xy = y * 4 + x
    place = y * 8 + x * 2 + core

    def device(x_, y_, z_, core_):
        return (y_ * 8 + lax.rem(z_, 4) * 2 + core_, x_ * 2 + z_ // 4)

    def member(p):
        return device(lax.rem(p // 2, 4), p // 8, z, lax.rem(p, 2))

    def same(device_):
        return (device_[0] == pen) & (device_[1] == chan)

    z_index = [lax.rem(z + d, 8) for d in range(1, 8)]
    z_peers = [device(x, y, i, core) for i in z_index]
    xy_index = [lax.rem(xy + d, 16) for d in range(1, 16)]
    xy_peers = [device(lax.rem(i, 4), i // 4, z, core) for i in xy_index]
    y_index = [lax.rem(y + d, 4) for d in range(1, 4)]
    y_peers = [device(x, i, z, core) for i in y_index]
    order = [(2, 2), (2, 1), (2, 3), (1, 2), (3, 2), (2, 0), (0, 2), (1, 1), (3, 3), (1, 3), (3, 1)]
    order += [(1, 0), (3, 0), (0, 1), (0, 3), (0, 0)]
    place_index = [
        lax.rem(y + dy, 4) * 8 + lax.rem(x + dx, 4) * 2 + lax.rem(core + dc, 2)
        for dx, dy in order
        for dc in (0, 1)
        if (dx, dy, dc) != (0, 0, 0)
    ]
    place_peers = [member(p) for p in place_index]
    sibling = device(x, y, z, 1 - core)
    x_index = [lax.rem(x + d, 4) for d in range(1, 4)]
    x_peers = [device(i, y, z, core) for i in x_index]
    z_partner = device(x, y, (1 - zhi) * 4 + zlo, core)
    to_index = [lax.rem(z + d, 8) for d in (4, 1, 7, 2, 6, 3, 5, 0)]
    to_devices = [device(zlo, y, i, core) for i in to_index]
    from_devices = [device(i // 2, y, (i % 2) * 4 + x, core) for i in range(8)]

    reads = []
    for g in range(3):
        part = pl.ds(g * 4, 4)
        for n, (src, dst) in enumerate(((lat_hbm, lat_ref), (cot_hbm, cot_ref))):
            reads.append(pltpu.make_async_copy(src.at[part], dst.at[part], io_sem.at[g * 2 + n]))
            reads[-1].start()
    loads = []
    for n, (src, dst) in enumerate(zip(const_hbm, const)):
        load = pltpu.make_async_copy(src, dst, const_sem.at[n])
        load.start()
        loads.append(load)
    loads = dict(zip(CONSTS, loads))

    barrier = pltpu.get_barrier_semaphore()
    for peer in place_peers + z_peers:
        pl.semaphore_signal(barrier, inc=1, device_id=peer, device_id_type=MESH)
    for peer in from_devices:

        @pl.when(jnp.logical_not(same(peer)))
        def _():
            pl.semaphore_signal(barrier, inc=1, device_id=peer, device_id_type=MESH)

    zsrc[0:4, :] = win_ref[...].astype(F32)
    zsrc[4:8, :] = wout_ref[...].astype(F32)
    zbuf[z] = zsrc[...]
    fsrc[...] = jnp.concatenate(
        [ff_ref[0].astype(F32), ff_ref[1].astype(F32), fs_ref[0].astype(F32), fs_ref[1].astype(F32)],
        axis=1,
    )
    fpair[zhi] = fsrc[...]
    normed_s[:, 176:192, :] = jnp.zeros((LAT, 16, 256), BF16)
    cot_s[:, 176:192, :] = jnp.zeros((LAT, 16, 256), BF16)
    own = jnp.where(x == zlo, 1, 0)
    pl.semaphore_wait(barrier, len(place_peers) + len(z_peers) + 8 - own)

    w_z = Push(wzs, wzr)
    for peer in z_peers:
        w_z.start(zsrc, zbuf.at[z], peer)
    f_p = Push(fps, fpr)
    f_p.start(fsrc, fpair.at[zhi], z_partner)

    loads["basis_t"].wait()

    def ex1_copy(g, n):
        return remote(
            send1.at[g, to_index[n]],
            recv1.at[g, chan],
            s1s.at[g, n],
            s1r.at[g, chan],
            to_devices[n],
        )

    def ex1_start(g):
        reads[2 * g].wait()
        reads[2 * g + 1].wait()

        def row(l, carry):
            i = g * 4 + l
            cot_s[i, 0:SEG] = cot_ref[i]
            values = lat_ref[i].astype(F32)
            centred = values - jnp.mean(values, axis=-1, keepdims=True)
            spread = jnp.mean(centred * centred, axis=-1, keepdims=True)
            normed_s[i, 0:SEG] = (centred * lax.rsqrt(spread + 1e-05) * gain_ref[...]).astype(BF16)
            return carry

        lax.fori_loop(0, 4, row, 0)
        for slot, rows in enumerate((normed_s, cot_s)):
            coded = [dot(Vt[...], rows[g * 4 + l]) for l in range(4)]
            for b in range(8):
                part = jnp.concatenate([c[:, 32 * b : 32 * b + 32] for c in coded], axis=1)
                send1[g, b, slot] = part.astype(BF16)
        for n in range(8):

            @pl.when(jnp.logical_not(same(to_devices[n])))
            def _():
                ex1_copy(g, n).start()

        @pl.when(x == zlo)
        def _():
            recv1[g, chan] = send1[g, z]

    def ex1_wait(g):
        for i in range(8):

            @pl.when(jnp.logical_not(same(from_devices[i])))
            def _():
                remote(
                    send1.at[g, i], recv1.at[g, i], s1s.at[g, i], s1r.at[g, i], from_devices[i]
                ).wait_recv()

    def ex1_sent(g):
        for n in range(8):

            @pl.when(jnp.logical_not(same(to_devices[n])))
            def _():
                ex1_copy(g, n).wait_send()

    ex1_start(0)
    w_z.wait_recv()
    pk[0] = jnp.concatenate([zbuf[i, 0:4] for i in range(8)], axis=0).astype(BF16)
    pk[1] = jnp.concatenate([zbuf[i, 4:8] for i in range(8)], axis=0).astype(BF16)
    wfull[core, xy] = pk[...]
    w_x = Push(wxs, wxr)
    for peer in x_peers:
        w_x.start(pk, wfull.at[core, xy], peer)
    f_p.wait_recv()
    fall[x] = fpair[...]
    f_a = Push(fas, far)
    for peer in x_peers:
        f_a.start(fpair, fall.at[x], peer)
    ex1_start(1)
    ex1_start(2)

    w_x.wait_recv()
    w_y = Push(wys, wyr)
    own_y = pl.ds(y * 4, 4)
    for peer in y_peers:
        w_y.start(wfull.at[core, own_y], wfull.at[core, own_y], peer)
    w_y.wait_recv()
    w_c = Push(wcs, wcr)
    w_c.start(wfull.at[core], wfull.at[core], sibling)
    cm_s[...] = jnp.zeros_like(cm_s)
    dc_s[...] = jnp.zeros_like(dc_s)
    gacc[...] = jnp.zeros_like(gacc)
    w_c.wait_recv()

    def mlp_step(i, carry):
        t, h = i // 4, lax.rem(i, 4)
        half, part = h // 2, pl.ds(lax.rem(h, 2) * 8, 8)
        rows = pl.ds(t * 4, 4)
        tokens = normed_s[rows].reshape(4 * PAD, 256)
        grads = cot_s[rows].reshape(4 * PAD, 256)
        w_in = wfull[half, part, 0].reshape(256, 256)
        w_out = wfull[half, part, 1].reshape(256, 256)
        value, slope = gelu_parts(dot(tokens, w_in, 1, 1))
        hidden = value.astype(BF16)
        d_pre = (dot(grads, w_out, 1, 1) * slope).astype(BF16)
        cm_s[rows] += dot(hidden, w_out).reshape(4, PAD, 256)
        dc_s[rows] += dot(d_pre, w_in).reshape(4, PAD, 256)
        gacc[half, part, 0] += dot(d_pre, tokens, 0, 0).reshape(8, 32, 256)
        gacc[half, part, 1] += dot(hidden, grads, 0, 0).reshape(8, 32, 256)
        return carry

    row = lax.broadcasted_iota(jnp.int32, (768, 1), 0)
    weight = jnp.where((row == 0) | (row == 12), 1.0, 2.0).astype(F32)

    def pair_rows(modes):
        both = [modes[:, :128].reshape(32, 24, 128), modes[:, 128:].reshape(32, 24, 128)]
        return jnp.concatenate(both, axis=1).astype(BF16)

    def split_rows(ref, g):
        both = ref[g].astype(F32)
        return both[:, :24].reshape(768, 128), both[:, 24:].reshape(768, 128)

    def swap(send, recv, send_sem, recv_sem, g):
        push = Push(send_sem.at[g], recv_sem.at[g])
        for index, peer in zip(place_index, place_peers):
            push.start(send.at[g, index], recv.at[g, place], peer)
        recv[g, place] = send[g, place]
        return push

    def zonal(g):
        ex1_wait(g)
        coded = jnp.concatenate(
            [jnp.concatenate([recv1[g, i, 0], recv1[g, i, 1]], axis=1) for i in range(8)], axis=0
        )
        modes = dot(expand[...], coded)
        modes = jnp.concatenate([modes[:, :128], modes[:, 128:] * weight], axis=1)
        send2[g] = pair_rows(modes)
        return swap(send2, recv2, s2s, s2r, g)

    loads["expand"].wait()
    ex2 = [None] * 3
    lax.fori_loop(0, 2, mlp_step, 0)
    ex2[0] = zonal(0)
    lax.fori_loop(2, 7, mlp_step, 0)
    ex2[1] = zonal(1)
    lax.fori_loop(7, 12, mlp_step, 0)
    gsc[...] = gacc[1 - core].astype(BF16)
    g_c = Push(gcs, gcr)
    g_c.start(gsc, grc, sibling)
    ex2[2] = zonal(2)

    r128 = lax.broadcasted_iota(jnp.int32, (128, 128), 0) // 32
    c128 = lax.broadcasted_iota(jnp.int32, (128, 128), 1) // 32
    block = (r128 == c128).astype(F32)
    lane_group = lax.broadcasted_iota(jnp.int32, (32, 128), 1) // 32

    def over_groups(tile):
        tile = tile + pltpu.roll(tile, 64, 1)
        return tile + pltpu.roll(tile, 32, 1)

    f_a.wait_recv()
    filters = fall[z // 2, lax.rem(z, 2)]

    def spread_filter(n):
        parts = []
        for part in range(2):
            w = over_groups(jnp.where(lane_group == 2 * n + part, filters, 0.0))
            parts.append(jnp.concatenate([w] * 4, axis=0) * block)
        re, im = parts
        top = jnp.concatenate([re, im], axis=1)
        low = jnp.concatenate([-im, re], axis=1)
        return jnp.concatenate([top, low], axis=0).astype(BF16)

    filter_1 = spread_filter(0)
    filter_2 = spread_filter(1)
    for name in CONSTS[2:]:
        loads[name].wait()

    def meridian_first(g):
        ex2[g].wait_recv()
        lanes = slice(g * 128, g * 128 + 128)
        modes = jnp.concatenate(split_rows(recv2, g), axis=1).astype(BF16)
        out = dot(first[...], modes)
        for slot in range(2):
            re = out[:384, slot * 128 : slot * 128 + 128]
            im = out[384:, slot * 128 : slot * 128 + 128]
            mixed_s[slot, :, lanes] = (re * tw_re[:, lanes] - im * tw_im[:, lanes]).astype(BF16)
            mixed_s[slot, :, 384 + g * 128 : 512 + g * 128] = (
                re * tw_im[:, lanes] + im * tw_re[:, lanes]
            ).astype(BF16)

    def meridian_second(slot):
        out = dot(mixed_s[slot], second[...])
        return jnp.concatenate(
            [
                jnp.concatenate(
                    [out[:, g * 128 : g * 128 + 128], out[:, 384 + g * 128 : 512 + g * 128]], axis=1
                )
                for g in range(3)
            ],
            axis=0,
        )

    def meridian_back(spectra):
        spectra = jnp.concatenate(
            [spectra[g * 384 : g * 384 + 384, :128] for g in range(3)]
            + [spectra[g * 384 : g * 384 + 384, 128:] for g in range(3)],
            axis=1,
        )
        out = dot(spectra, second_t[...])
        re, im = out[:, :384], out[:, 384:]
        h_re = re * tw_re[...] + im * tw_im[...]
        h_im = im * tw_re[...] - re * tw_im[...]
        return jnp.concatenate([h_re, h_im], axis=0).astype(BF16)

    meridian_first(0)
    meridian_first(1)

    g_c.wait_recv()
    gsy[...] = (gacc[core] + grc[...].astype(F32)).astype(BF16)
    g_y = Push(gys, gyr)
    for index, peer in zip(y_index, y_peers):
        g_y.start(gsy.at[pl.ds(index * 4, 4)], gry.at[y], peer)
    gry[y] = gsy[own_y]

    meridian_first(2)
    spectrum = meridian_second(0).astype(BF16)
    value, slope = gelu_parts(dot(spectrum, filter_1))
    first_hidden = value.astype(BF16)
    second_act = dot(first_hidden, filter_2)
    bend = jnp.tanh(second_act * 10.0)
    shrunk = (second_act - 0.1 * bend).astype(BF16)
    d_second = (meridian_second(1) * bend * bend).astype(BF16)
    d_first = (dot(d_second, filter_2, 1, 1) * slope).astype(BF16)
    d_spectrum = dot(d_first, filter_1, 1, 1).astype(BF16)
    back_0 = meridian_back(shrunk)
    back_1 = meridian_back(d_spectrum)
    ex3 = []
    for g in range(3):
        lanes = slice(g * 128, g * 128 + 128)
        both = jnp.concatenate([back_0[:, lanes], back_1[:, lanes]], axis=1)
        send3[g] = pair_rows(dot(first_t[...], both))
        ex3.append(swap(send3, recv3, s3s, s3r, g))

    def fold(outer):
        o = {}
        for p in range(2):
            for q in range(2):
                tile = outer[p * 128 : p * 128 + 128, q * 128 : q * 128 + 128] * block
                o[p, q] = over_groups(tile[0:32] + tile[32:64] + tile[64:96] + tile[96:128])
        return o[0, 0] + o[1, 1], o[0, 1] - o[1, 0]

    f1_re, f1_im = fold(dot(spectrum, d_first, 0, 0))
    f2_re, f2_im = fold(dot(first_hidden, d_second, 0, 0))
    fbuf[0] = jnp.where(
        lane_group == 0, f1_re, jnp.where(lane_group == 1, f1_im, jnp.where(lane_group == 2, f2_re, f2_im))
    )
    f_c = Push(fcs, fcr)
    f_c.start(fbuf.at[0], frc, sibling)

    def unzonal(g):
        ex3[g].wait_recv()
        modes_0, modes_1 = split_rows(recv3, g)
        modes = jnp.concatenate([modes_0 * weight, modes_1], axis=1).astype(BF16)
        coded = dot(expand_t[...], modes)
        for i in range(8):
            for slot in range(2):
                part = coded[i * RANK : i * RANK + RANK, slot * 128 : slot * 128 + 128]
                send4[g, i // 2, i % 2, slot] = part.astype(BF16)
        push = Push(s4s.at[g], s4r.at[g])
        for index, peer in zip(x_index, x_peers):
            push.start(send4.at[g, index], mid4.at[g, x], peer)
        mid4[g, x] = send4[g, x]
        onward(g, 0)
        return push

    def ex5_copy(g, d, h):
        xs = lax.rem(x + (0, 3, 2, 1)[d], 4)
        to = h * 4 + xs
        copy = remote(
            mid4.at[g, xs, h],
            recv4.at[g, z],
            s5s.at[g, d * 2 + h],
            s5r.at[g, z],
            device(x, y, to, core),
        )
        return copy, to, xs

    def onward(g, d):
        for h in range(2):
            copy, to, xs = ex5_copy(g, d, h)

            @pl.when(to != z)
            def _():
                copy.start()

            @pl.when(to == z)
            def _():
                recv4[g, z] = mid4[g, xs, h]

    def forward(g):
        for d in range(1, 4):
            ex4[g].copies[d - 1].wait_recv()
            onward(g, d)

    def ex5_wait(g):
        for i in z_index:
            remote(
                mid4.at[g, 0, 0], recv4.at[g, i], s5s.at[g, 0], s5r.at[g, i], device(x, y, i, core)
            ).wait_recv()

    ex4 = [None] * 3
    ex4[0] = unzonal(0)
    f_c.wait_recv()
    fbuf[1] = fbuf[0] + frc[...]
    f_x = Push(fxs, fxr)
    for peer in xy_peers:
        f_x.start(fbuf.at[1], frx.at[xy], peer)
    frx[xy] = fbuf[1]
    g_y.wait_recv()
    gsx[...] = (
        (gry[0].astype(F32) + gry[1].astype(F32)) + (gry[2].astype(F32) + gry[3].astype(F32))
    ).astype(BF16)
    g_x = Push(gxs, gxr)
    for index, peer in zip(x_index, x_peers):
        g_x.start(gsx.at[index], grx.at[x], peer)
    grx[x] = gsx[x]
    ex4[1] = unzonal(1)
    forward(0)
    ex4[2] = unzonal(2)
    forward(1)

    g_x.wait_recv()
    summed = grx[0].astype(F32)
    for i in range(1, 4):
        summed = summed + grx[i].astype(F32)
    for i in range(8):
        gsz[i, 0:4] = summed[0, i * 4 : i * 4 + 4]
        gsz[i, 4:8] = summed[1, i * 4 : i * 4 + 4]
    g_z = Push(gzs, gzr)
    for index, peer in zip(z_index, z_peers):
        g_z.start(gsz.at[index], grz.at[z], peer)
    grz[z] = gsz[z]
    f_x.wait_recv()
    total = frx[0]
    for i in range(1, 16):
        total = total + frx[i]
    fbuf[2] = total
    f_z = Push(fzs, fzr)
    for peer in z_peers:
        f_z.start(fbuf.at[2], frz.at[z], peer)
    frz[z] = fbuf[2]
    forward(2)

    g_z.wait_recv()
    total = grz[0]
    for i in range(1, 8):
        total = total + grz[i]
    gwi_ref[...] = total[0:4]
    gwo_ref[...] = total[4:8]
    f_z.wait_recv()
    total = frz[chan]
    gff_ref[0] = total[:, 0:32]
    gff_ref[1] = total[:, 32:64]
    gfs_ref[0] = total[:, 64:96]
    gfs_ref[1] = total[:, 96:128]

    writes = []

    def finish(g):
        ex5_wait(g)

        for l in range(4):
            i = g * 4 + l
            lanes = slice(32 * l, 32 * l + 32)
            values = lat_ref[i].astype(F32)
            coded = jnp.concatenate([recv4[g, b, 0][:, lanes] for b in range(8)], axis=1)
            spatial = dot(V[...], coded)[:SEG]
            bo_ref[i] = (values + spatial + cm_s[i, 0:SEG]).astype(BF16)
            coded = jnp.concatenate([recv4[g, b, 1][:, lanes] for b in range(8)], axis=1)
            d_normed = dot(V[...], coded)[:SEG] + dc_s[i, 0:SEG]
            centred = values - jnp.mean(values, axis=-1, keepdims=True)
            spread = jnp.mean(centred * centred, axis=-1, keepdims=True)
            scale = lax.rsqrt(spread + 1e-05)
            unit = centred * scale
            d_unit = d_normed * gain_ref[...]
            mean_d = jnp.mean(d_unit, axis=-1, keepdims=True)
            mean_du = jnp.mean(d_unit * unit, axis=-1, keepdims=True)
            d_values = scale * (d_unit - mean_d - unit * mean_du)
            gl_ref[i] = (cot_ref[i].astype(F32) + d_values).astype(BF16)
        part = pl.ds(g * 4, 4)
        for n, (src, dst) in enumerate(((bo_ref, bo_hbm), (gl_ref, gl_hbm))):
            write = pltpu.make_async_copy(src.at[part], dst.at[part], io_sem.at[6 + g * 2 + n])
            write.start()
            writes.append(write)

    for g in range(3):
        finish(g)

    for write in writes:
        write.wait()
    for push in [w_z, w_x, w_y, w_c, g_c, g_y, g_x, g_z, f_p, f_a, f_c, f_x, f_z] + ex2 + ex3 + ex4:
        push.wait_send()
    for g in range(3):
        ex1_sent(g)
        for d in range(4):
            for h in range(2):
                copy, to, xs = ex5_copy(g, d, h)

                @pl.when(to != z)
                def _():
                    copy.wait_send()


def body(latents, norm_gain, weight_in, weight_out, filter_first, filter_second, cotangent):
    table = tables()
    consts = [jnp.asarray(table[name]) for name in CONSTS]
    dma = pltpu.SemaphoreType.DMA
    vmem = pl.BlockSpec(memory_space=pltpu.VMEM)
    hbm = pl.BlockSpec(memory_space=pl.ANY)
    scratch = [pltpu.VMEM(latents.shape, BF16)] * 4 + [dma((12,))]
    scratch += [pltpu.VMEM(c.shape, c.dtype) for c in consts]
    scratch += [
        pltpu.VMEM((LAT, PAD, 256), BF16),
        pltpu.VMEM((LAT, PAD, 256), BF16),
        pltpu.VMEM((3, 8, 2, RANK, 128), BF16),
        pltpu.VMEM((3, 8, 2, RANK, 128), BF16),
        pltpu.VMEM((3, 32, 48, 128), BF16),
        pltpu.VMEM((3, 32, 48, 128), BF16),
        pltpu.VMEM((3, 32, 48, 128), BF16),
        pltpu.VMEM((3, 32, 48, 128), BF16),
        pltpu.VMEM((3, 4, 2, 2, RANK, 128), BF16),
        pltpu.VMEM((3, 4, 2, 2, RANK, 128), BF16),
        pltpu.VMEM((3, 8, 2, RANK, 128), BF16),
        pltpu.VMEM((2, 384, 768), BF16),
        pltpu.VMEM((LAT, PAD, 256), F32),
        pltpu.VMEM((LAT, PAD, 256), F32),
        pltpu.VMEM((8, 256), F32),
        pltpu.VMEM((8, 8, 256), F32),
        pltpu.VMEM((2, 32, 256), BF16),
        pltpu.VMEM((2, 16, 2, 32, 256), BF16),
        pltpu.VMEM((2, 16, 2, 32, 256), F32),
        pltpu.VMEM((16, 2, 32, 256), BF16),
        pltpu.VMEM((16, 2, 32, 256), BF16),
        pltpu.VMEM((16, 2, 32, 256), BF16),
        pltpu.VMEM((4, 4, 2, 32, 256), BF16),
        pltpu.VMEM((4, 2, 32, 256), BF16),
        pltpu.VMEM((4, 2, 32, 256), BF16),
        pltpu.VMEM((8, 8, 256), F32),
        pltpu.VMEM((8, 8, 256), F32),
        pltpu.VMEM((32, 128), F32),
        pltpu.VMEM((2, 32, 128), F32),
        pltpu.VMEM((4, 2, 32, 128), F32),
        pltpu.VMEM((3, 32, 128), F32),
        pltpu.VMEM((32, 128), F32),
        pltpu.VMEM((16, 32, 128), F32),
        pltpu.VMEM((8, 32, 128), F32),
    ]
    scratch += [dma((len(CONSTS),))]
    for n in (8, 31, 31, 3, 8):
        scratch += [dma((3, n)), dma((3, n))]
    for n in (7, 3, 3, 1, 7, 3, 3, 1, 1, 3, 1, 15, 7):
        scratch += [dma((n,)), dma((n,))]
    out_shape = (
        jax.ShapeDtypeStruct(latents.shape, BF16),
        jax.ShapeDtypeStruct(latents.shape, BF16),
        jax.ShapeDtypeStruct((4, 256), F32),
        jax.ShapeDtypeStruct((4, 256), F32),
        jax.ShapeDtypeStruct((2, 32, 32), F32),
        jax.ShapeDtypeStruct((2, 32, 32), F32),
    )
    outs = pl.pallas_call(
        kernel,
        out_shape=out_shape,
        in_specs=[hbm] + [vmem] * 5 + [hbm] * (1 + len(CONSTS)),
        out_specs=(hbm,) * 2 + (vmem,) * 4,
        scratch_shapes=scratch,
        compiler_params=pltpu.CompilerParams(
            collective_id=0, has_side_effects=True, vmem_limit_bytes=62 * 1024 * 1024
        ),
        name="spectral_block",
    )(
        latents,
        norm_gain.reshape(1, 256),
        weight_in,
        weight_out,
        filter_first.reshape(2, 32, 32),
        filter_second.reshape(2, 32, 32),
        cotangent,
        *consts,
    )
    return outs[:4] + (outs[4].reshape(2, 1, 32, 32), outs[5].reshape(2, 1, 32, 32))


def solution(mesh):
    placed = (
        P("pen", "chan", None),
        P(),
        P(("pen", "chan"), None),
        P(("pen", "chan"), None),
        P(None, "chan", None, None),
        P(None, "chan", None, None),
        P("pen", "chan", None),
    )
    return jax.shard_map(
        body,
        mesh=mesh,
        in_specs=placed,
        out_specs=(
            P("pen", "chan", None),
            P("pen", "chan", None),
            P(("pen", "chan"), None),
            P(("pen", "chan"), None),
            P(None, "chan", None, None),
            P(None, "chan", None, None),
        ),
        check_vma=False,
    )
```

```python
import functools
import math

import jax
import jax.numpy as jnp
import ml_dtypes
import numpy as np
from jax import lax
from jax.experimental import pallas as pl
from jax.experimental.pallas import tpu as pltpu
from jax.sharding import PartitionSpec as P

MESH = pl.DeviceIdType.MESH
NLON, KLON, NLAT = 1440, 384, 384
SEG = 180
PAD = 192
RANK = 112
LAT = 12
NK = 12
GELU_C = math.sqrt(2.0 / math.pi)
F32, BF16 = jnp.float32, jnp.bfloat16


def as_bf16(values):
    return np.asarray(values, np.float32).astype(ml_dtypes.bfloat16)


@functools.lru_cache(None)
def tables():
    j = np.arange(NLON)[:, None]
    k = np.arange(KLON)[None, :]
    a = 2.0 * np.pi * ((j * k) % NLON) / NLON
    full = np.concatenate([np.cos(a), -np.sin(a)], axis=1) / math.sqrt(NLON)
    left, _, _ = np.linalg.svd(full[:SEG], full_matrices=False)
    basis = left[:, :RANK]
    expand = np.stack([basis.T @ full[s * SEG : (s + 1) * SEG] for s in range(8)])
    expand = expand.reshape(8, RANK, 2, 32, NK).transpose(3, 2, 4, 0, 1).reshape(768, 8 * RANK)
    basis_pad = np.zeros((PAD, RANK))
    basis_pad[:SEG] = basis
    s = np.arange(32)
    w32 = np.exp(-2j * np.pi * np.outer(s, s) / 32)
    l = np.arange(12)
    w12 = np.exp(-2j * np.pi * np.outer(l, l) / 12)

    def real_form(w):
        return np.stack(
            [np.stack([w.real, -w.imag], axis=1), np.stack([w.imag, w.real], axis=1)]
        )

    first = np.einsum("qmps,kl->qmkspl", real_form(w32), np.eye(NK)).reshape(768, 768)
    second = np.einsum("qmpl,cd->plcqmd", real_form(w12), np.eye(32)).reshape(768, 768)
    twiddle = np.exp(-2j * np.pi * np.outer(s, l) / 384) / math.sqrt(NLAT)
    twiddle = np.repeat(np.repeat(twiddle, NK, axis=0), 32, axis=1)
    return dict(
        basis=as_bf16(basis_pad),
        basis_t=as_bf16(basis_pad.T),
        expand=as_bf16(expand),
        expand_t=as_bf16(expand.T),
        first=as_bf16(first),
        first_t=as_bf16(first.T),
        second=as_bf16(second),
        second_t=as_bf16(second.T),
        tw_re=np.asarray(twiddle.real, np.float32),
        tw_im=np.asarray(twiddle.imag, np.float32),
    )


CONSTS = ("basis_t", "expand", "first", "tw_re", "tw_im", "second", "second_t", "first_t", "expand_t", "basis")


def dot(a, b, ca=1, cb=0):
    return lax.dot_general(a, b, (((ca,), (cb,)), ((), ())), preferred_element_type=F32)


def gelu_parts(v):
    v2 = v * v
    t = jnp.tanh(v * (GELU_C + (GELU_C * 0.044715) * v2))
    half = 0.5 + 0.5 * t
    value = v * half
    slope = half + (0.5 * v) * (1.0 - t * t) * (GELU_C + (3.0 * GELU_C * 0.044715) * v2)
    return value, slope


class Push:
    def __init__(self, send_sem, recv_sem):
        self.send_sem, self.recv_sem, self.copies = send_sem, recv_sem, []

    def start(self, src, dst, device):
        n = len(self.copies)
        copy = remote(src, dst, self.send_sem.at[n], self.recv_sem.at[n], device)
        copy.start()
        self.copies.append(copy)

    def wait_recv(self):
        for copy in self.copies:
            copy.wait_recv()

    def wait_send(self):
        for copy in self.copies:
            copy.wait_send()


def remote(src, dst, send_sem, recv_sem, device):
    return pltpu.make_async_remote_copy(
        src_ref=src,
        dst_ref=dst,
        send_sem=send_sem,
        recv_sem=recv_sem,
        device_id=device,
        device_id_type=MESH,
    )


def kernel(*refs):
    (lat_hbm, gain_ref, win_ref, wout_ref, ff_ref, fs_ref, cot_hbm) = refs[:7]
    const_hbm = refs[7 : 7 + len(CONSTS)]
    refs = refs[7 + len(CONSTS) :]
    (fields_hbm, gw_ref, gf_ref) = refs[:3]
    bo_hbm, gl_hbm = fields_hbm.at[0], fields_hbm.at[1]
    (lat_ref, cot_ref, bo_ref, gl_ref, io_sem) = refs[3:8]
    refs = refs[8:]
    const = refs[: len(CONSTS)]
    refs = refs[len(CONSTS) :]
    (normed_s, cot_s, send1, recv1, send2, recv2, send3, recv3, send4, mid4, recv4) = refs[:11]
    (mixed_s, cm_s, dc_s, zsrc, zbuf, pk, wfull, gacc, gsc, grc, gsy, gry, gsx) = refs[11:24]
    (grx, gsz, grz) = refs[24:27]
    refs = refs[2:]
    (fsrc, fpair, fall, fbuf, frc, frx, frz) = refs[25:32]
    (const_sem, s1s, s1r, s2s, s2r, s3s, s3r, s4s, s4r, s5s, s5r) = refs[32:43]
    (wzs, wzr, wxs, wxr, wys, wyr, wcs, wcr) = refs[43:51]
    (gzs, gzr, gxs, gxr, gys, gyr, gcs, gcr) = refs[51:59]
    (fps, fpr, fas, far, fcs, fcr, fxs, fxr, fzs, fzr) = refs[59:69]
    Vt, expand, first, tw_re, tw_im, second, second_t, first_t, expand_t, V = const

    pen = lax.axis_index("pen")
    chan = lax.axis_index("chan")
    x, zhi = chan // 2, lax.rem(chan, 2)
    y, zlo, core = pen // 8, lax.rem(pen // 2, 4), lax.rem(pen, 2)
    z = zhi * 4 + zlo
    xy = y * 4 + x
    place = y * 8 + x * 2 + core

    def device(x_, y_, z_, core_):
        return (y_ * 8 + lax.rem(z_, 4) * 2 + core_, x_ * 2 + z_ // 4)

    def member(p):
        return device(lax.rem(p // 2, 4), p // 8, z, lax.rem(p, 2))

    def same(device_):
        return (device_[0] == pen) & (device_[1] == chan)

    z_index = [lax.rem(z + d, 8) for d in range(1, 8)]
    z_peers = [device(x, y, i, core) for i in z_index]
    xy_index = [lax.rem(xy + d, 16) for d in range(1, 16)]
    xy_peers = [device(lax.rem(i, 4), i // 4, z, core) for i in xy_index]
    y_index = [lax.rem(y + d, 4) for d in range(1, 4)]
    y_peers = [device(x, i, z, core) for i in y_index]
    order = [(2, 2), (2, 1), (2, 3), (1, 2), (3, 2), (2, 0), (0, 2), (1, 1), (3, 3), (1, 3), (3, 1)]
    order += [(1, 0), (3, 0), (0, 1), (0, 3), (0, 0)]
    place_index = [
        lax.rem(y + dy, 4) * 8 + lax.rem(x + dx, 4) * 2 + lax.rem(core + dc, 2)
        for dx, dy in order
        for dc in (0, 1)
        if (dx, dy, dc) != (0, 0, 0)
    ]
    place_peers = [member(p) for p in place_index]
    sibling = device(x, y, z, 1 - core)
    x_index = [lax.rem(x + d, 4) for d in range(1, 4)]
    x_peers = [device(i, y, z, core) for i in x_index]
    z_partner = device(x, y, (1 - zhi) * 4 + zlo, core)
    to_index = [lax.rem(z + d, 8) for d in (4, 1, 7, 2, 6, 3, 5, 0)]
    to_devices = [device(zlo, y, i, core) for i in to_index]
    from_devices = [device(i // 2, y, (i % 2) * 4 + x, core) for i in range(8)]

    reads = []
    for g in range(3):
        part = pl.ds(g * 4, 4)
        for n, (src, dst) in enumerate(((lat_hbm, lat_ref), (cot_hbm, cot_ref))):
            reads.append(pltpu.make_async_copy(src.at[part], dst.at[part], io_sem.at[g * 2 + n]))
            reads[-1].start()
    loads = []
    for n, (src, dst) in enumerate(zip(const_hbm, const)):
        load = pltpu.make_async_copy(src, dst, const_sem.at[n])
        load.start()
        loads.append(load)
    loads = dict(zip(CONSTS, loads))

    barrier = pltpu.get_barrier_semaphore()
    for peer in place_peers + z_peers:
        pl.semaphore_signal(barrier, inc=1, device_id=peer, device_id_type=MESH)
    for peer in from_devices:

        @pl.when(jnp.logical_not(same(peer)))
        def _():
            pl.semaphore_signal(barrier, inc=1, device_id=peer, device_id_type=MESH)

    zsrc[0:4, :] = win_ref[...].astype(F32)
    zsrc[4:8, :] = wout_ref[...].astype(F32)
    zbuf[z] = zsrc[...]
    fsrc[...] = jnp.concatenate(
        [ff_ref[0].astype(F32), ff_ref[1].astype(F32), fs_ref[0].astype(F32), fs_ref[1].astype(F32)],
        axis=1,
    )
    fpair[zhi] = fsrc[...]
    normed_s[:, 176:192, :] = jnp.zeros((LAT, 16, 256), BF16)
    cot_s[:, 176:192, :] = jnp.zeros((LAT, 16, 256), BF16)
    own = jnp.where(x == zlo, 1, 0)
    pl.semaphore_wait(barrier, len(place_peers) + len(z_peers) + 8 - own)

    w_z = Push(wzs, wzr)
    for peer in z_peers:
        w_z.start(zsrc, zbuf.at[z], peer)
    f_p = Push(fps, fpr)
    f_p.start(fsrc, fpair.at[zhi], z_partner)

    loads["basis_t"].wait()

    def ex1_copy(g, n):
        return remote(
            send1.at[g, to_index[n]],
            recv1.at[g, chan],
            s1s.at[g, n],
            s1r.at[g, chan],
            to_devices[n],
        )

    def ex1_start(g):
        reads[2 * g].wait()
        reads[2 * g + 1].wait()

        def row(l, carry):
            i = g * 4 + l
            cot_s[i, 0:SEG] = cot_ref[i]
            values = lat_ref[i].astype(F32)
            centred = values - jnp.mean(values, axis=-1, keepdims=True)
            spread = jnp.mean(centred * centred, axis=-1, keepdims=True)
            normed_s[i, 0:SEG] = (centred * lax.rsqrt(spread + 1e-05) * gain_ref[...]).astype(BF16)
            return carry

        lax.fori_loop(0, 4, row, 0)
        for slot, rows in enumerate((normed_s, cot_s)):
            coded = [dot(Vt[...], rows[g * 4 + l]) for l in range(4)]
            for b in range(8):
                part = jnp.concatenate([c[:, 32 * b : 32 * b + 32] for c in coded], axis=1)
                send1[g, b, slot] = part.astype(BF16)
        for n in range(8):

            @pl.when(jnp.logical_not(same(to_devices[n])))
            def _():
                ex1_copy(g, n).start()

        @pl.when(x == zlo)
        def _():
            recv1[g, chan] = send1[g, z]

    def ex1_wait(g):
        for i in range(8):

            @pl.when(jnp.logical_not(same(from_devices[i])))
            def _():
                remote(
                    send1.at[g, i], recv1.at[g, i], s1s.at[g, i], s1r.at[g, i], from_devices[i]
                ).wait_recv()

    def ex1_sent(g):
        for n in range(8):

            @pl.when(jnp.logical_not(same(to_devices[n])))
            def _():
                ex1_copy(g, n).wait_send()

    ex1_start(0)
    w_z.wait_recv()
    pk[0] = jnp.concatenate([zbuf[i, 0:4] for i in range(8)], axis=0).astype(BF16)
    pk[1] = jnp.concatenate([zbuf[i, 4:8] for i in range(8)], axis=0).astype(BF16)
    wfull[core, xy] = pk[...]
    w_x = Push(wxs, wxr)
    for peer in x_peers:
        w_x.start(pk, wfull.at[core, xy], peer)
    f_p.wait_recv()
    fall[x] = fpair[...]
    f_a = Push(fas, far)
    for peer in x_peers:
        f_a.start(fpair, fall.at[x], peer)
    ex1_start(1)
    ex1_start(2)

    w_x.wait_recv()
    w_y = Push(wys, wyr)
    own_y = pl.ds(y * 4, 4)
    for peer in y_peers:
        w_y.start(wfull.at[core, own_y], wfull.at[core, own_y], peer)
    w_y.wait_recv()
    w_c = Push(wcs, wcr)
    w_c.start(wfull.at[core], wfull.at[core], sibling)
    cm_s[...] = jnp.zeros_like(cm_s)
    dc_s[...] = jnp.zeros_like(dc_s)
    gacc[...] = jnp.zeros_like(gacc)
    w_c.wait_recv()

    def mlp_step(i, carry):
        t, h = i // 4, lax.rem(i, 4)
        half, part = h // 2, pl.ds(lax.rem(h, 2) * 8, 8)
        rows = pl.ds(t * 4, 4)
        tokens = normed_s[rows].reshape(4 * PAD, 256)
        grads = cot_s[rows].reshape(4 * PAD, 256)
        w_in = wfull[half, part, 0].reshape(256, 256)
        w_out = wfull[half, part, 1].reshape(256, 256)
        value, slope = gelu_parts(dot(tokens, w_in, 1, 1))
        hidden = value.astype(BF16)
        d_pre = (dot(grads, w_out, 1, 1) * slope).astype(BF16)
        cm_s[rows] += dot(hidden, w_out).reshape(4, PAD, 256)
        dc_s[rows] += dot(d_pre, w_in).reshape(4, PAD, 256)
        gacc[half, part, 0] += dot(d_pre, tokens, 0, 0).reshape(8, 32, 256)
        gacc[half, part, 1] += dot(hidden, grads, 0, 0).reshape(8, 32, 256)
        return carry

    row = lax.broadcasted_iota(jnp.int32, (768, 1), 0)
    weight = jnp.where((row == 0) | (row == 12), 1.0, 2.0).astype(F32)

    def pair_rows(modes):
        both = [modes[:, :128].reshape(32, 24, 128), modes[:, 128:].reshape(32, 24, 128)]
        return jnp.concatenate(both, axis=1).astype(BF16)

    def split_rows(ref, g):
        both = ref[g].astype(F32)
        return both[:, :24].reshape(768, 128), both[:, 24:].reshape(768, 128)

    def swap(send, recv, send_sem, recv_sem, g):
        push = Push(send_sem.at[g], recv_sem.at[g])
        for index, peer in zip(place_index, place_peers):
            push.start(send.at[g, index], recv.at[g, place], peer)
        recv[g, place] = send[g, place]
        return push

    def zonal(g):
        ex1_wait(g)
        coded = jnp.concatenate(
            [jnp.concatenate([recv1[g, i, 0], recv1[g, i, 1]], axis=1) for i in range(8)], axis=0
        )
        modes = dot(expand[...], coded)
        modes = jnp.concatenate([modes[:, :128], modes[:, 128:] * weight], axis=1)
        send2[g] = pair_rows(modes)
        return swap(send2, recv2, s2s, s2r, g)

    loads["expand"].wait()
    ex2 = [None] * 3
    lax.fori_loop(0, 2, mlp_step, 0)
    ex2[0] = zonal(0)
    lax.fori_loop(2, 6, mlp_step, 0)
    ex2[1] = zonal(1)
    lax.fori_loop(6, 9, mlp_step, 0)
    ex2[2] = zonal(2)
    lax.fori_loop(9, 12, mlp_step, 0)
    gsc[...] = gacc[1 - core].astype(BF16)
    g_c = Push(gcs, gcr)
    g_c.start(gsc, grc, sibling)

    r128 = lax.broadcasted_iota(jnp.int32, (128, 128), 0) // 32
    c128 = lax.broadcasted_iota(jnp.int32, (128, 128), 1) // 32
    block = (r128 == c128).astype(F32)
    lane_group = lax.broadcasted_iota(jnp.int32, (32, 128), 1) // 32

    def over_groups(tile):
        tile = tile + pltpu.roll(tile, 64, 1)
        return tile + pltpu.roll(tile, 32, 1)

    f_a.wait_recv()
    filters = fall[z // 2, lax.rem(z, 2)]

    def spread_filter(n):
        parts = []
        for part in range(2):
            w = over_groups(jnp.where(lane_group == 2 * n + part, filters, 0.0))
            parts.append(jnp.concatenate([w] * 4, axis=0) * block)
        re, im = parts
        top = jnp.concatenate([re, im], axis=1)
        low = jnp.concatenate([-im, re], axis=1)
        return jnp.concatenate([top, low], axis=0).astype(BF16)

    filter_1 = spread_filter(0)
    filter_2 = spread_filter(1)
    for name in CONSTS[2:]:
        loads[name].wait()

    def meridian_first(g):
        ex2[g].wait_recv()
        lanes = slice(g * 128, g * 128 + 128)
        modes = jnp.concatenate(split_rows(recv2, g), axis=1).astype(BF16)
        out = dot(first[...], modes)
        for slot in range(2):
            re = out[:384, slot * 128 : slot * 128 + 128]
            im = out[384:, slot * 128 : slot * 128 + 128]
            mixed_s[slot, :, lanes] = (re * tw_re[:, lanes] - im * tw_im[:, lanes]).astype(BF16)
            mixed_s[slot, :, 384 + g * 128 : 512 + g * 128] = (
                re * tw_im[:, lanes] + im * tw_re[:, lanes]
            ).astype(BF16)

    def meridian_second(slot):
        out = dot(mixed_s[slot], second[...])
        return jnp.concatenate(
            [
                jnp.concatenate(
                    [out[:, g * 128 : g * 128 + 128], out[:, 384 + g * 128 : 512 + g * 128]], axis=1
                )
                for g in range(3)
            ],
            axis=0,
        )

    def meridian_back(spectra):
        spectra = jnp.concatenate(
            [spectra[g * 384 : g * 384 + 384, :128] for g in range(3)]
            + [spectra[g * 384 : g * 384 + 384, 128:] for g in range(3)],
            axis=1,
        )
        out = dot(spectra, second_t[...])
        re, im = out[:, :384], out[:, 384:]
        h_re = re * tw_re[...] + im * tw_im[...]
        h_im = im * tw_re[...] - re * tw_im[...]
        return jnp.concatenate([h_re, h_im], axis=0).astype(BF16)

    meridian_first(0)
    meridian_first(1)

    meridian_first(2)
    spectrum = meridian_second(0).astype(BF16)
    value, slope = gelu_parts(dot(spectrum, filter_1))
    first_hidden = value.astype(BF16)
    second_act = dot(first_hidden, filter_2)
    bend = jnp.tanh(second_act * 10.0)
    shrunk = (second_act - 0.1 * bend).astype(BF16)
    d_second = (meridian_second(1) * bend * bend).astype(BF16)
    d_first = (dot(d_second, filter_2, 1, 1) * slope).astype(BF16)
    d_spectrum = dot(d_first, filter_1, 1, 1).astype(BF16)
    back_0 = meridian_back(shrunk)
    back_1 = meridian_back(d_spectrum)
    ex3 = []
    for g in range(3):
        lanes = slice(g * 128, g * 128 + 128)
        both = jnp.concatenate([back_0[:, lanes], back_1[:, lanes]], axis=1)
        send3[g] = pair_rows(dot(first_t[...], both))
        ex3.append(swap(send3, recv3, s3s, s3r, g))

    def fold(outer):
        o = {}
        for p in range(2):
            for q in range(2):
                tile = outer[p * 128 : p * 128 + 128, q * 128 : q * 128 + 128] * block
                o[p, q] = over_groups(tile[0:32] + tile[32:64] + tile[64:96] + tile[96:128])
        return o[0, 0] + o[1, 1], o[0, 1] - o[1, 0]

    f1_re, f1_im = fold(dot(spectrum, d_first, 0, 0))
    f2_re, f2_im = fold(dot(first_hidden, d_second, 0, 0))
    fbuf[0] = jnp.where(
        lane_group == 0, f1_re, jnp.where(lane_group == 1, f1_im, jnp.where(lane_group == 2, f2_re, f2_im))
    )
    f_c = Push(fcs, fcr)
    f_c.start(fbuf.at[0], frc, sibling)

    def unzonal(g):
        ex3[g].wait_recv()
        modes_0, modes_1 = split_rows(recv3, g)
        modes = jnp.concatenate([modes_0 * weight, modes_1], axis=1).astype(BF16)
        coded = dot(expand_t[...], modes)
        for i in range(8):
            for slot in range(2):
                part = coded[i * RANK : i * RANK + RANK, slot * 128 : slot * 128 + 128]
                send4[g, i // 2, i % 2, slot] = part.astype(BF16)
        push = Push(s4s.at[g], s4r.at[g])
        for index, peer in zip(x_index, x_peers):
            push.start(send4.at[g, index], mid4.at[g, x], peer)
        mid4[g, x] = send4[g, x]
        onward(g, 0)
        return push

    def ex5_copy(g, d, h):
        xs = lax.rem(x + (0, 3, 2, 1)[d], 4)
        to = h * 4 + xs
        copy = remote(
            mid4.at[g, xs, h],
            recv4.at[g, z],
            s5s.at[g, d * 2 + h],
            s5r.at[g, z],
            device(x, y, to, core),
        )
        return copy, to, xs

    def onward(g, d):
        for h in range(2):
            copy, to, xs = ex5_copy(g, d, h)

            @pl.when(to != z)
            def _():
                copy.start()

            @pl.when(to == z)
            def _():
                recv4[g, z] = mid4[g, xs, h]

    def forward(g):
        for d in range(1, 4):
            ex4[g].copies[d - 1].wait_recv()
            onward(g, d)

    def ex5_wait(g):
        for i in z_index:
            remote(
                mid4.at[g, 0, 0], recv4.at[g, i], s5s.at[g, 0], s5r.at[g, i], device(x, y, i, core)
            ).wait_recv()

    ex4 = [None] * 3
    g_c.wait_recv()
    gsy[...] = (gacc[core] + grc[...].astype(F32)).astype(BF16)
    g_y = Push(gys, gyr)
    for index, peer in zip(y_index, y_peers):
        g_y.start(gsy.at[pl.ds(index * 4, 4)], gry.at[y], peer)
    gry[y] = gsy[own_y]

    ex4[0] = unzonal(0)
    ex4[1] = unzonal(1)
    forward(0)
    ex4[2] = unzonal(2)
    f_c.wait_recv()
    fbuf[1] = fbuf[0] + frc[...]
    f_x = Push(fxs, fxr)
    for peer in xy_peers:
        f_x.start(fbuf.at[1], frx.at[xy], peer)
    frx[xy] = fbuf[1]

    g_y.wait_recv()
    gsx[...] = (
        (gry[0].astype(F32) + gry[1].astype(F32)) + (gry[2].astype(F32) + gry[3].astype(F32))
    ).astype(BF16)
    g_x = Push(gxs, gxr)
    for index, peer in zip(x_index, x_peers):
        g_x.start(gsx.at[index], grx.at[x], peer)
    grx[x] = gsx[x]

    forward(1)
    forward(2)

    g_x.wait_recv()
    summed = grx[0].astype(F32)
    for i in range(1, 4):
        summed = summed + grx[i].astype(F32)
    for i in range(8):
        gsz[i, 0:4] = summed[0, i * 4 : i * 4 + 4]
        gsz[i, 4:8] = summed[1, i * 4 : i * 4 + 4]
    g_z = Push(gzs, gzr)
    for index, peer in zip(z_index, z_peers):
        g_z.start(gsz.at[index], grz.at[z], peer)
    grz[z] = gsz[z]

    f_x.wait_recv()
    total = frx[0]
    for i in range(1, 16):
        total = total + frx[i]
    fbuf[2] = total
    f_z = Push(fzs, fzr)
    for peer in z_peers:
        f_z.start(fbuf.at[2], frz.at[z], peer)
    frz[z] = fbuf[2]

    writes = []

    def finish(g):
        ex5_wait(g)

        for l in range(4):
            i = g * 4 + l
            lanes = slice(32 * l, 32 * l + 32)
            values = lat_ref[i].astype(F32)
            coded = jnp.concatenate([recv4[g, b, 0][:, lanes] for b in range(8)], axis=1)
            spatial = dot(V[...], coded)[:SEG]
            bo_ref[i] = (values + spatial + cm_s[i, 0:SEG]).astype(BF16)
            coded = jnp.concatenate([recv4[g, b, 1][:, lanes] for b in range(8)], axis=1)
            d_normed = dot(V[...], coded)[:SEG] + dc_s[i, 0:SEG]
            centred = values - jnp.mean(values, axis=-1, keepdims=True)
            spread = jnp.mean(centred * centred, axis=-1, keepdims=True)
            scale = lax.rsqrt(spread + 1e-05)
            unit = centred * scale
            d_unit = d_normed * gain_ref[...]
            mean_d = jnp.mean(d_unit, axis=-1, keepdims=True)
            mean_du = jnp.mean(d_unit * unit, axis=-1, keepdims=True)
            d_values = scale * (d_unit - mean_d - unit * mean_du)
            gl_ref[i] = (cot_ref[i].astype(F32) + d_values).astype(BF16)
        part = pl.ds(g * 4, 4)
        for n, (src, dst) in enumerate(((bo_ref, bo_hbm), (gl_ref, gl_hbm))):
            write = pltpu.make_async_copy(src.at[part], dst.at[part], io_sem.at[6 + g * 2 + n])
            write.start()
            writes.append(write)

    finish(0)
    finish(1)
    g_z.wait_recv()
    total = grz[0]
    for i in range(1, 8):
        total = total + grz[i]
    gw_ref[0] = total[0:4]
    gw_ref[1] = total[4:8]
    f_z.wait_recv()
    total = frz[chan]
    for n in range(2):
        for part in range(2):
            lo = n * 64 + part * 32
            gf_ref[n, part] = total[:, lo : lo + 32]

    finish(2)

    for write in writes:
        write.wait()
    for push in [w_z, w_x, w_y, w_c, g_c, g_y, g_x, g_z, f_p, f_a, f_c, f_x, f_z] + ex2 + ex3 + ex4:
        push.wait_send()
    for g in range(3):
        ex1_sent(g)
        for d in range(4):
            for h in range(2):
                copy, to, xs = ex5_copy(g, d, h)

                @pl.when(to != z)
                def _():
                    copy.wait_send()


def body(latents, norm_gain, weight_in, weight_out, filter_first, filter_second, cotangent):
    table = tables()
    consts = [jnp.asarray(table[name]) for name in CONSTS]
    dma = pltpu.SemaphoreType.DMA
    vmem = pl.BlockSpec(memory_space=pltpu.VMEM)
    hbm = pl.BlockSpec(memory_space=pl.ANY)
    scratch = [pltpu.VMEM(latents.shape, BF16)] * 4 + [dma((12,))]
    scratch += [pltpu.VMEM(c.shape, c.dtype) for c in consts]
    scratch += [
        pltpu.VMEM((LAT, PAD, 256), BF16),
        pltpu.VMEM((LAT, PAD, 256), BF16),
        pltpu.VMEM((3, 8, 2, RANK, 128), BF16),
        pltpu.VMEM((3, 8, 2, RANK, 128), BF16),
        pltpu.VMEM((3, 32, 48, 128), BF16),
        pltpu.VMEM((3, 32, 48, 128), BF16),
        pltpu.VMEM((3, 32, 48, 128), BF16),
        pltpu.VMEM((3, 32, 48, 128), BF16),
        pltpu.VMEM((3, 4, 2, 2, RANK, 128), BF16),
        pltpu.VMEM((3, 4, 2, 2, RANK, 128), BF16),
        pltpu.VMEM((3, 8, 2, RANK, 128), BF16),
        pltpu.VMEM((2, 384, 768), BF16),
        pltpu.VMEM((LAT, PAD, 256), F32),
        pltpu.VMEM((LAT, PAD, 256), F32),
        pltpu.VMEM((8, 256), F32),
        pltpu.VMEM((8, 8, 256), F32),
        pltpu.VMEM((2, 32, 256), BF16),
        pltpu.VMEM((2, 16, 2, 32, 256), BF16),
        pltpu.VMEM((2, 16, 2, 32, 256), F32),
        pltpu.VMEM((16, 2, 32, 256), BF16),
        pltpu.VMEM((16, 2, 32, 256), BF16),
        pltpu.VMEM((16, 2, 32, 256), BF16),
        pltpu.VMEM((4, 4, 2, 32, 256), BF16),
        pltpu.VMEM((4, 2, 32, 256), BF16),
        pltpu.VMEM((4, 2, 32, 256), BF16),
        pltpu.VMEM((8, 8, 256), F32),
        pltpu.VMEM((8, 8, 256), F32),
        pltpu.VMEM((32, 128), F32),
        pltpu.VMEM((2, 32, 128), F32),
        pltpu.VMEM((4, 2, 32, 128), F32),
        pltpu.VMEM((3, 32, 128), F32),
        pltpu.VMEM((32, 128), F32),
        pltpu.VMEM((16, 32, 128), F32),
        pltpu.VMEM((8, 32, 128), F32),
    ]
    scratch += [dma((len(CONSTS),))]
    for n in (8, 31, 31, 3, 8):
        scratch += [dma((3, n)), dma((3, n))]
    for n in (7, 3, 3, 1, 7, 3, 3, 1, 1, 3, 1, 15, 7):
        scratch += [dma((n,)), dma((n,))]
    out_shape = (
        jax.ShapeDtypeStruct((2,) + latents.shape, BF16),
        jax.ShapeDtypeStruct((2, 4, 256), F32),
        jax.ShapeDtypeStruct((2, 2, 32, 32), F32),
    )
    outs = pl.pallas_call(
        kernel,
        out_shape=out_shape,
        in_specs=[hbm] + [vmem] * 5 + [hbm] * (1 + len(CONSTS)),
        out_specs=(hbm,) + (vmem,) * 2,
        scratch_shapes=scratch,
        compiler_params=pltpu.CompilerParams(
            collective_id=0, has_side_effects=True, vmem_limit_bytes=62 * 1024 * 1024
        ),
        name="spectral_block",
    )(
        latents,
        norm_gain.reshape(1, 256),
        weight_in,
        weight_out,
        filter_first.reshape(2, 32, 32),
        filter_second.reshape(2, 32, 32),
        cotangent,
        *consts,
    )
    fields, weights, filters = outs
    filters = filters.reshape(2, 2, 1, 32, 32)
    return fields[0], fields[1], weights[0], weights[1], filters[0], filters[1]


def solution(mesh):
    placed = (
        P("pen", "chan", None),
        P(),
        P(("pen", "chan"), None),
        P(("pen", "chan"), None),
        P(None, "chan", None, None),
        P(None, "chan", None, None),
        P("pen", "chan", None),
    )
    return jax.shard_map(
        body,
        mesh=mesh,
        in_specs=placed,
        out_specs=(
            P("pen", "chan", None),
            P("pen", "chan", None),
            P(("pen", "chan"), None),
            P(("pen", "chan"), None),
            P(None, "chan", None, None),
            P(None, "chan", None, None),
        ),
        check_vma=False,
    )
```

```python
import functools
import math

import jax
import jax.numpy as jnp
import ml_dtypes
import numpy as np
from jax import lax
from jax.experimental import pallas as pl
from jax.experimental.pallas import tpu as pltpu
from jax.sharding import PartitionSpec as P

MESH = pl.DeviceIdType.MESH
NLON, KLON, NLAT = 1440, 384, 384
SEG = 180
PAD = 192
RANK = 112
LAT = 12
NK = 12
GELU_C = math.sqrt(2.0 / math.pi)
F32, BF16 = jnp.float32, jnp.bfloat16


def as_bf16(values):
    return np.asarray(values, np.float32).astype(ml_dtypes.bfloat16)


@functools.lru_cache(None)
def tables():
    j = np.arange(NLON)[:, None]
    k = np.arange(KLON)[None, :]
    a = 2.0 * np.pi * ((j * k) % NLON) / NLON
    full = np.concatenate([np.cos(a), -np.sin(a)], axis=1) / math.sqrt(NLON)
    left, _, _ = np.linalg.svd(full[:SEG], full_matrices=False)
    basis = left[:, :RANK]
    expand = np.stack([basis.T @ full[s * SEG : (s + 1) * SEG] for s in range(8)])
    expand = expand.reshape(8, RANK, 2, 32, NK).transpose(3, 2, 4, 0, 1).reshape(768, 8 * RANK)
    basis_pad = np.zeros((PAD, RANK))
    basis_pad[:SEG] = basis
    s = np.arange(32)
    w32 = np.exp(-2j * np.pi * np.outer(s, s) / 32)
    l = np.arange(12)
    w12 = np.exp(-2j * np.pi * np.outer(l, l) / 12)

    def real_form(w):
        return np.stack(
            [np.stack([w.real, -w.imag], axis=1), np.stack([w.imag, w.real], axis=1)]
        )

    first = np.einsum("qmps,kl->qmkspl", real_form(w32), np.eye(NK)).reshape(768, 768)
    second = np.einsum("qmpl,cd->plcqmd", real_form(w12), np.eye(32)).reshape(768, 768)
    twiddle = np.exp(-2j * np.pi * np.outer(s, l) / 384) / math.sqrt(NLAT)
    twiddle = np.repeat(np.repeat(twiddle, NK, axis=0), 32, axis=1)
    return dict(
        basis=as_bf16(basis_pad),
        basis_t=as_bf16(basis_pad.T),
        expand=as_bf16(expand),
        expand_t=as_bf16(expand.T),
        first=as_bf16(first),
        first_t=as_bf16(first.T),
        second=as_bf16(second),
        second_t=as_bf16(second.T),
        tw_re=np.asarray(twiddle.real, np.float32),
        tw_im=np.asarray(twiddle.imag, np.float32),
    )


CONSTS = ("basis_t", "expand", "first", "tw_re", "tw_im", "second", "second_t", "first_t", "expand_t", "basis")


def dot(a, b, ca=1, cb=0):
    return lax.dot_general(a, b, (((ca,), (cb,)), ((), ())), preferred_element_type=F32)


def gelu_parts(v):
    v2 = v * v
    t = jnp.tanh(v * (GELU_C + (GELU_C * 0.044715) * v2))
    half = 0.5 + 0.5 * t
    value = v * half
    slope = half + (0.5 * v) * (1.0 - t * t) * (GELU_C + (3.0 * GELU_C * 0.044715) * v2)
    return value, slope


class Push:
    def __init__(self, send_sem, recv_sem):
        self.send_sem, self.recv_sem, self.copies = send_sem, recv_sem, []

    def start(self, src, dst, device):
        n = len(self.copies)
        copy = remote(src, dst, self.send_sem.at[n], self.recv_sem.at[n], device)
        copy.start()
        self.copies.append(copy)

    def wait_recv(self):
        for copy in self.copies:
            copy.wait_recv()

    def wait_send(self):
        for copy in self.copies:
            copy.wait_send()


def remote(src, dst, send_sem, recv_sem, device):
    return pltpu.make_async_remote_copy(
        src_ref=src,
        dst_ref=dst,
        send_sem=send_sem,
        recv_sem=recv_sem,
        device_id=device,
        device_id_type=MESH,
    )


def kernel(*refs):
    (lat_hbm, gain_ref, win_ref, wout_ref, ff_ref, fs_ref, cot_hbm) = refs[:7]
    const_hbm = refs[7 : 7 + len(CONSTS)]
    refs = refs[7 + len(CONSTS) :]
    (fields_hbm, gw_ref, gf_ref) = refs[:3]
    bo_hbm, gl_hbm = fields_hbm.at[0], fields_hbm.at[1]
    (lat_ref, cot_ref, bo_ref, gl_ref, io_sem) = refs[3:8]
    refs = refs[8:]
    const = refs[: len(CONSTS)]
    refs = refs[len(CONSTS) :]
    (normed_s, cot_s, send1, recv1, send2, recv2, send3, recv3, send4, mid4, recv4) = refs[:11]
    (mixed_s, cm_s, dc_s, zsrc, zbuf, pk, wfull, gacc, gsc, grc, gsy, gry, gsx) = refs[11:24]
    (grx, gsz, grz) = refs[24:27]
    refs = refs[2:]
    (fsrc, fpair, fall, fbuf, frc, frx, frz) = refs[25:32]
    (const_sem, s1s, s1r, s2s, s2r, s3s, s3r, s4s, s4r, s5s, s5r) = refs[32:43]
    (wzs, wzr, wxs, wxr, wys, wyr, wcs, wcr) = refs[43:51]
    (gzs, gzr, gxs, gxr, gys, gyr, gcs, gcr) = refs[51:59]
    (fps, fpr, fas, far, fcs, fcr, fxs, fxr, fzs, fzr) = refs[59:69]
    Vt, expand, first, tw_re, tw_im, second, second_t, first_t, expand_t, V = const

    pen = lax.axis_index("pen")
    chan = lax.axis_index("chan")
    x, zhi = chan // 2, lax.rem(chan, 2)
    y, zlo, core = pen // 8, lax.rem(pen // 2, 4), lax.rem(pen, 2)
    z = zhi * 4 + zlo
    xy = y * 4 + x
    place = y * 8 + x * 2 + core

    def device(x_, y_, z_, core_):
        return (y_ * 8 + lax.rem(z_, 4) * 2 + core_, x_ * 2 + z_ // 4)

    def member(p):
        return device(lax.rem(p // 2, 4), p // 8, z, lax.rem(p, 2))

    def same(device_):
        return (device_[0] == pen) & (device_[1] == chan)

    z_index = [lax.rem(z + d, 8) for d in range(1, 8)]
    z_peers = [device(x, y, i, core) for i in z_index]
    xy_index = [lax.rem(xy + d, 16) for d in range(1, 16)]
    xy_peers = [device(lax.rem(i, 4), i // 4, z, core) for i in xy_index]
    y_index = [lax.rem(y + d, 4) for d in range(1, 4)]
    y_peers = [device(x, i, z, core) for i in y_index]
    order = [(2, 2), (2, 1), (2, 3), (1, 2), (3, 2), (2, 0), (0, 2), (1, 1), (3, 3), (1, 3), (3, 1)]
    order += [(1, 0), (3, 0), (0, 1), (0, 3), (0, 0)]
    place_index = [
        lax.rem(y + dy, 4) * 8 + lax.rem(x + dx, 4) * 2 + lax.rem(core + dc, 2)
        for dx, dy in order
        for dc in (0, 1)
        if (dx, dy, dc) != (0, 0, 0)
    ]
    place_peers = [member(p) for p in place_index]
    sibling = device(x, y, z, 1 - core)
    x_index = [lax.rem(x + d, 4) for d in range(1, 4)]
    x_peers = [device(i, y, z, core) for i in x_index]
    z_partner = device(x, y, (1 - zhi) * 4 + zlo, core)
    to_index = [lax.rem(z + d, 8) for d in (4, 1, 7, 2, 6, 3, 5, 0)]
    to_devices = [device(zlo, y, i, core) for i in to_index]
    from_devices = [device(i // 2, y, (i % 2) * 4 + x, core) for i in range(8)]

    reads = []
    for g in range(3):
        part = pl.ds(g * 4, 4)
        for n, (src, dst) in enumerate(((lat_hbm, lat_ref), (cot_hbm, cot_ref))):
            reads.append(pltpu.make_async_copy(src.at[part], dst.at[part], io_sem.at[g * 2 + n]))
            reads[-1].start()
    barrier = pltpu.get_barrier_semaphore()
    for peer in place_peers + z_peers:
        pl.semaphore_signal(barrier, inc=1, device_id=peer, device_id_type=MESH)
    for peer in from_devices:

        @pl.when(jnp.logical_not(same(peer)))
        def _():
            pl.semaphore_signal(barrier, inc=1, device_id=peer, device_id_type=MESH)

    loads = []
    for n, (src, dst) in enumerate(zip(const_hbm, const)):
        load = pltpu.make_async_copy(src, dst, const_sem.at[n])
        load.start()
        loads.append(load)
    loads = dict(zip(CONSTS, loads))

    zsrc[0:4, :] = win_ref[...].astype(F32)
    zsrc[4:8, :] = wout_ref[...].astype(F32)
    zbuf[z] = zsrc[...]
    fsrc[...] = jnp.concatenate(
        [ff_ref[0].astype(F32), ff_ref[1].astype(F32), fs_ref[0].astype(F32), fs_ref[1].astype(F32)],
        axis=1,
    )
    fpair[zhi] = fsrc[...]
    normed_s[:, 176:192, :] = jnp.zeros((LAT, 16, 256), BF16)
    cot_s[:, 176:192, :] = jnp.zeros((LAT, 16, 256), BF16)
    own = jnp.where(x == zlo, 1, 0)
    pl.semaphore_wait(barrier, len(place_peers) + len(z_peers) + 8 - own)

    w_z = Push(wzs, wzr)
    for peer in z_peers:
        w_z.start(zsrc, zbuf.at[z], peer)
    f_p = Push(fps, fpr)
    f_p.start(fsrc, fpair.at[zhi], z_partner)

    loads["basis_t"].wait()

    def ex1_copy(g, n):
        return remote(
            send1.at[g, to_index[n]],
            recv1.at[g, chan],
            s1s.at[g, n],
            s1r.at[g, chan],
            to_devices[n],
        )

    def ex1_start(g):
        reads[2 * g].wait()
        reads[2 * g + 1].wait()

        def row(l, carry):
            i = g * 4 + l
            cot_s[i, 0:SEG] = cot_ref[i]
            values = lat_ref[i].astype(F32)
            centred = values - jnp.mean(values, axis=-1, keepdims=True)
            spread = jnp.mean(centred * centred, axis=-1, keepdims=True)
            normed_s[i, 0:SEG] = (centred * lax.rsqrt(spread + 1e-05) * gain_ref[...]).astype(BF16)
            return carry

        lax.fori_loop(0, 4, row, 0)
        for slot, rows in enumerate((normed_s, cot_s)):
            coded = [dot(Vt[...], rows[g * 4 + l]) for l in range(4)]
            for b in range(8):
                part = jnp.concatenate([c[:, 32 * b : 32 * b + 32] for c in coded], axis=1)
                send1[g, b, slot] = part.astype(BF16)
        for n in range(8):

            @pl.when(jnp.logical_not(same(to_devices[n])))
            def _():
                ex1_copy(g, n).start()

        @pl.when(x == zlo)
        def _():
            recv1[g, chan] = send1[g, z]

    def ex1_wait(g):
        for i in range(8):

            @pl.when(jnp.logical_not(same(from_devices[i])))
            def _():
                remote(
                    send1.at[g, i], recv1.at[g, i], s1s.at[g, i], s1r.at[g, i], from_devices[i]
                ).wait_recv()

    def ex1_sent(g):
        for n in range(8):

            @pl.when(jnp.logical_not(same(to_devices[n])))
            def _():
                ex1_copy(g, n).wait_send()

    ex1_start(0)
    w_z.wait_recv()
    pk[0] = jnp.concatenate([zbuf[i, 0:4] for i in range(8)], axis=0).astype(BF16)
    pk[1] = jnp.concatenate([zbuf[i, 4:8] for i in range(8)], axis=0).astype(BF16)
    wfull[core, xy] = pk[...]
    w_x = Push(wxs, wxr)
    for peer in x_peers:
        w_x.start(pk, wfull.at[core, xy], peer)
    f_p.wait_recv()
    fall[x] = fpair[...]
    f_a = Push(fas, far)
    for peer in x_peers:
        f_a.start(fpair, fall.at[x], peer)
    ex1_start(1)
    ex1_start(2)

    w_x.wait_recv()
    w_y = Push(wys, wyr)
    own_y = pl.ds(y * 4, 4)
    for peer in y_peers:
        w_y.start(wfull.at[core, own_y], wfull.at[core, own_y], peer)
    w_y.wait_recv()
    w_c = Push(wcs, wcr)
    w_c.start(wfull.at[core], wfull.at[core], sibling)
    cm_s[...] = jnp.zeros_like(cm_s)
    dc_s[...] = jnp.zeros_like(dc_s)
    gacc[...] = jnp.zeros_like(gacc)
    w_c.wait_recv()

    def mlp_step(i, carry):
        t, h = i // 4, lax.rem(i, 4)
        half, part = h // 2, pl.ds(lax.rem(h, 2) * 8, 8)
        rows = pl.ds(t * 4, 4)
        tokens = normed_s[rows].reshape(4 * PAD, 256)
        grads = cot_s[rows].reshape(4 * PAD, 256)
        w_in = wfull[half, part, 0].reshape(256, 256)
        w_out = wfull[half, part, 1].reshape(256, 256)
        value, slope = gelu_parts(dot(tokens, w_in, 1, 1))
        hidden = value.astype(BF16)
        d_pre = (dot(grads, w_out, 1, 1) * slope).astype(BF16)
        cm_s[rows] += dot(hidden, w_out).reshape(4, PAD, 256)
        dc_s[rows] += dot(d_pre, w_in).reshape(4, PAD, 256)
        gacc[half, part, 0] += dot(d_pre, tokens, 0, 0).reshape(8, 32, 256)
        gacc[half, part, 1] += dot(hidden, grads, 0, 0).reshape(8, 32, 256)
        return carry

    row = lax.broadcasted_iota(jnp.int32, (768, 1), 0)
    weight = jnp.where((row == 0) | (row == 12), 1.0, 2.0).astype(F32)

    def pair_rows(modes):
        both = [modes[:, :128].reshape(32, 24, 128), modes[:, 128:].reshape(32, 24, 128)]
        return jnp.concatenate(both, axis=1).astype(BF16)

    def split_rows(ref, g):
        both = ref[g].astype(F32)
        return both[:, :24].reshape(768, 128), both[:, 24:].reshape(768, 128)

    def swap(send, recv, send_sem, recv_sem, g):
        push = Push(send_sem.at[g], recv_sem.at[g])
        for index, peer in zip(place_index, place_peers):
            push.start(send.at[g, index], recv.at[g, place], peer)
        recv[g, place] = send[g, place]
        return push

    def zonal(g):
        ex1_wait(g)
        coded = jnp.concatenate(
            [jnp.concatenate([recv1[g, i, 0], recv1[g, i, 1]], axis=1) for i in range(8)], axis=0
        )
        modes = dot(expand[...], coded)
        modes = jnp.concatenate([modes[:, :128], modes[:, 128:] * weight], axis=1)
        send2[g] = pair_rows(modes)
        return swap(send2, recv2, s2s, s2r, g)

    loads["expand"].wait()
    ex2 = [None] * 3
    lax.fori_loop(0, 2, mlp_step, 0)
    ex2[0] = zonal(0)
    lax.fori_loop(2, 6, mlp_step, 0)
    ex2[1] = zonal(1)
    lax.fori_loop(6, 9, mlp_step, 0)
    ex2[2] = zonal(2)
    lax.fori_loop(9, 12, mlp_step, 0)
    gsc[...] = gacc[1 - core].astype(BF16)
    g_c = Push(gcs, gcr)
    g_c.start(gsc, grc, sibling)

    r128 = lax.broadcasted_iota(jnp.int32, (128, 128), 0) // 32
    c128 = lax.broadcasted_iota(jnp.int32, (128, 128), 1) // 32
    block = (r128 == c128).astype(F32)
    lane_group = lax.broadcasted_iota(jnp.int32, (32, 128), 1) // 32

    def over_groups(tile):
        tile = tile + pltpu.roll(tile, 64, 1)
        return tile + pltpu.roll(tile, 32, 1)

    f_a.wait_recv()
    filters = fall[z // 2, lax.rem(z, 2)]

    def spread_filter(n):
        parts = []
        for part in range(2):
            w = over_groups(jnp.where(lane_group == 2 * n + part, filters, 0.0))
            parts.append(jnp.concatenate([w] * 4, axis=0) * block)
        re, im = parts
        top = jnp.concatenate([re, im], axis=1)
        low = jnp.concatenate([-im, re], axis=1)
        return jnp.concatenate([top, low], axis=0).astype(BF16)

    filter_1 = spread_filter(0)
    filter_2 = spread_filter(1)
    for name in CONSTS[2:]:
        loads[name].wait()

    def meridian_first(g):
        ex2[g].wait_recv()
        lanes = slice(g * 128, g * 128 + 128)
        modes = jnp.concatenate(split_rows(recv2, g), axis=1).astype(BF16)
        out = dot(first[...], modes)
        for slot in range(2):
            re = out[:384, slot * 128 : slot * 128 + 128]
            im = out[384:, slot * 128 : slot * 128 + 128]
            mixed_s[slot, :, lanes] = (re * tw_re[:, lanes] - im * tw_im[:, lanes]).astype(BF16)
            mixed_s[slot, :, 384 + g * 128 : 512 + g * 128] = (
                re * tw_im[:, lanes] + im * tw_re[:, lanes]
            ).astype(BF16)

    def meridian_second(slot):
        out = dot(mixed_s[slot], second[...])
        return jnp.concatenate(
            [
                jnp.concatenate(
                    [out[:, g * 128 : g * 128 + 128], out[:, 384 + g * 128 : 512 + g * 128]], axis=1
                )
                for g in range(3)
            ],
            axis=0,
        )

    def meridian_back(spectra):
        spectra = jnp.concatenate(
            [spectra[g * 384 : g * 384 + 384, :128] for g in range(3)]
            + [spectra[g * 384 : g * 384 + 384, 128:] for g in range(3)],
            axis=1,
        )
        out = dot(spectra, second_t[...])
        re, im = out[:, :384], out[:, 384:]
        h_re = re * tw_re[...] + im * tw_im[...]
        h_im = im * tw_re[...] - re * tw_im[...]
        return jnp.concatenate([h_re, h_im], axis=0).astype(BF16)

    meridian_first(0)
    meridian_first(1)

    meridian_first(2)
    spectrum = meridian_second(0).astype(BF16)
    value, slope = gelu_parts(dot(spectrum, filter_1))
    first_hidden = value.astype(BF16)
    second_act = dot(first_hidden, filter_2)
    bend = jnp.tanh(second_act * 10.0)
    shrunk = (second_act - 0.1 * bend).astype(BF16)
    d_second = (meridian_second(1) * bend * bend).astype(BF16)
    d_first = (dot(d_second, filter_2, 1, 1) * slope).astype(BF16)
    d_spectrum = dot(d_first, filter_1, 1, 1).astype(BF16)
    back_0 = meridian_back(shrunk)
    back_1 = meridian_back(d_spectrum)
    ex3 = []
    for g in range(3):
        lanes = slice(g * 128, g * 128 + 128)
        both = jnp.concatenate([back_0[:, lanes], back_1[:, lanes]], axis=1)
        send3[g] = pair_rows(dot(first_t[...], both))
        ex3.append(swap(send3, recv3, s3s, s3r, g))

    def fold(outer):
        o = {}
        for p in range(2):
            for q in range(2):
                tile = outer[p * 128 : p * 128 + 128, q * 128 : q * 128 + 128] * block
                o[p, q] = over_groups(tile[0:32] + tile[32:64] + tile[64:96] + tile[96:128])
        return o[0, 0] + o[1, 1], o[0, 1] - o[1, 0]

    f1_re, f1_im = fold(dot(spectrum, d_first, 0, 0))
    f2_re, f2_im = fold(dot(first_hidden, d_second, 0, 0))
    fbuf[0] = jnp.where(
        lane_group == 0, f1_re, jnp.where(lane_group == 1, f1_im, jnp.where(lane_group == 2, f2_re, f2_im))
    )
    f_c = Push(fcs, fcr)
    f_c.start(fbuf.at[0], frc, sibling)

    def unzonal(g):
        ex3[g].wait_recv()
        modes_0, modes_1 = split_rows(recv3, g)
        modes = jnp.concatenate([modes_0 * weight, modes_1], axis=1).astype(BF16)
        coded = dot(expand_t[...], modes)
        for i in range(8):
            for slot in range(2):
                part = coded[i * RANK : i * RANK + RANK, slot * 128 : slot * 128 + 128]
                send4[g, i // 2, i % 2, slot] = part.astype(BF16)
        push = Push(s4s.at[g], s4r.at[g])
        for index, peer in zip(x_index, x_peers):
            push.start(send4.at[g, index], mid4.at[g, x], peer)
        mid4[g, x] = send4[g, x]
        onward(g, 0)
        return push

    def ex5_copy(g, d, h):
        xs = lax.rem(x + (0, 3, 2, 1)[d], 4)
        to = h * 4 + xs
        copy = remote(
            mid4.at[g, xs, h],
            recv4.at[g, z],
            s5s.at[g, d * 2 + h],
            s5r.at[g, z],
            device(x, y, to, core),
        )
        return copy, to, xs

    def onward(g, d):
        for h in range(2):
            copy, to, xs = ex5_copy(g, d, h)

            @pl.when(to != z)
            def _():
                copy.start()

            @pl.when(to == z)
            def _():
                recv4[g, z] = mid4[g, xs, h]

    def forward(g):
        for d in range(1, 4):
            ex4[g].copies[d - 1].wait_recv()
            onward(g, d)

    def ex5_wait(g):
        for i in z_index:
            remote(
                mid4.at[g, 0, 0], recv4.at[g, i], s5s.at[g, 0], s5r.at[g, i], device(x, y, i, core)
            ).wait_recv()

    ex4 = [None] * 3
    g_c.wait_recv()
    gsy[...] = (gacc[core] + grc[...].astype(F32)).astype(BF16)
    g_y = Push(gys, gyr)
    for index, peer in zip(y_index, y_peers):
        g_y.start(gsy.at[pl.ds(index * 4, 4)], gry.at[y], peer)
    gry[y] = gsy[own_y]

    ex4[0] = unzonal(0)
    ex4[1] = unzonal(1)
    forward(0)
    ex4[2] = unzonal(2)
    f_c.wait_recv()
    fbuf[1] = fbuf[0] + frc[...]
    f_x = Push(fxs, fxr)
    for peer in xy_peers:
        f_x.start(fbuf.at[1], frx.at[xy], peer)
    frx[xy] = fbuf[1]

    g_y.wait_recv()
    gsx[...] = (
        (gry[0].astype(F32) + gry[1].astype(F32)) + (gry[2].astype(F32) + gry[3].astype(F32))
    ).astype(BF16)
    g_x = Push(gxs, gxr)
    for index, peer in zip(x_index, x_peers):
        g_x.start(gsx.at[index], grx.at[x], peer)
    grx[x] = gsx[x]

    forward(1)
    forward(2)

    g_x.wait_recv()
    summed = grx[0].astype(F32)
    for i in range(1, 4):
        summed = summed + grx[i].astype(F32)
    for i in range(8):
        gsz[i, 0:4] = summed[0, i * 4 : i * 4 + 4]
        gsz[i, 4:8] = summed[1, i * 4 : i * 4 + 4]
    g_z = Push(gzs, gzr)
    for index, peer in zip(z_index, z_peers):
        g_z.start(gsz.at[index], grz.at[z], peer)
    grz[z] = gsz[z]

    f_x.wait_recv()
    total = frx[0]
    for i in range(1, 16):
        total = total + frx[i]
    fbuf[2] = total
    f_z = Push(fzs, fzr)
    for peer in z_peers:
        f_z.start(fbuf.at[2], frz.at[z], peer)
    frz[z] = fbuf[2]

    writes = []

    def finish(g):
        ex5_wait(g)

        for l in range(4):
            i = g * 4 + l
            lanes = slice(32 * l, 32 * l + 32)
            values = lat_ref[i].astype(F32)
            coded = jnp.concatenate([recv4[g, b, 0][:, lanes] for b in range(8)], axis=1)
            spatial = dot(V[...], coded)[:SEG]
            bo_ref[i] = (values + spatial + cm_s[i, 0:SEG]).astype(BF16)
            coded = jnp.concatenate([recv4[g, b, 1][:, lanes] for b in range(8)], axis=1)
            d_normed = dot(V[...], coded)[:SEG] + dc_s[i, 0:SEG]
            centred = values - jnp.mean(values, axis=-1, keepdims=True)
            spread = jnp.mean(centred * centred, axis=-1, keepdims=True)
            scale = lax.rsqrt(spread + 1e-05)
            unit = centred * scale
            d_unit = d_normed * gain_ref[...]
            mean_d = jnp.mean(d_unit, axis=-1, keepdims=True)
            mean_du = jnp.mean(d_unit * unit, axis=-1, keepdims=True)
            d_values = scale * (d_unit - mean_d - unit * mean_du)
            gl_ref[i] = (cot_ref[i].astype(F32) + d_values).astype(BF16)
        part = pl.ds(g * 4, 4)
        for n, (src, dst) in enumerate(((bo_ref, bo_hbm), (gl_ref, gl_hbm))):
            write = pltpu.make_async_copy(src.at[part], dst.at[part], io_sem.at[6 + g * 2 + n])
            write.start()
            writes.append(write)

    finish(0)
    finish(1)
    g_z.wait_recv()
    total = grz[0]
    for i in range(1, 8):
        total = total + grz[i]
    gw_ref[0] = total[0:4]
    gw_ref[1] = total[4:8]
    f_z.wait_recv()
    total = frz[chan]
    for n in range(2):
        for part in range(2):
            lo = n * 64 + part * 32
            gf_ref[n, part] = total[:, lo : lo + 32]

    finish(2)

    for write in writes:
        write.wait()
    for push in [w_z, w_x, w_y, w_c, g_c, g_y, g_x, g_z, f_p, f_a, f_c, f_x, f_z] + ex2 + ex3 + ex4:
        push.wait_send()
    for g in range(3):
        ex1_sent(g)
        for d in range(4):
            for h in range(2):
                copy, to, xs = ex5_copy(g, d, h)

                @pl.when(to != z)
                def _():
                    copy.wait_send()


def body(latents, norm_gain, weight_in, weight_out, filter_first, filter_second, cotangent):
    table = tables()
    consts = [jnp.asarray(table[name]) for name in CONSTS]
    dma = pltpu.SemaphoreType.DMA
    vmem = pl.BlockSpec(memory_space=pltpu.VMEM)
    hbm = pl.BlockSpec(memory_space=pl.ANY)
    scratch = [pltpu.VMEM(latents.shape, BF16)] * 4 + [dma((12,))]
    scratch += [pltpu.VMEM(c.shape, c.dtype) for c in consts]
    scratch += [
        pltpu.VMEM((LAT, PAD, 256), BF16),
        pltpu.VMEM((LAT, PAD, 256), BF16),
        pltpu.VMEM((3, 8, 2, RANK, 128), BF16),
        pltpu.VMEM((3, 8, 2, RANK, 128), BF16),
        pltpu.VMEM((3, 32, 48, 128), BF16),
        pltpu.VMEM((3, 32, 48, 128), BF16),
        pltpu.VMEM((3, 32, 48, 128), BF16),
        pltpu.VMEM((3, 32, 48, 128), BF16),
        pltpu.VMEM((3, 4, 2, 2, RANK, 128), BF16),
        pltpu.VMEM((3, 4, 2, 2, RANK, 128), BF16),
        pltpu.VMEM((3, 8, 2, RANK, 128), BF16),
        pltpu.VMEM((2, 384, 768), BF16),
        pltpu.VMEM((LAT, PAD, 256), F32),
        pltpu.VMEM((LAT, PAD, 256), F32),
        pltpu.VMEM((8, 256), F32),
        pltpu.VMEM((8, 8, 256), F32),
        pltpu.VMEM((2, 32, 256), BF16),
        pltpu.VMEM((2, 16, 2, 32, 256), BF16),
        pltpu.VMEM((2, 16, 2, 32, 256), F32),
        pltpu.VMEM((16, 2, 32, 256), BF16),
        pltpu.VMEM((16, 2, 32, 256), BF16),
        pltpu.VMEM((16, 2, 32, 256), BF16),
        pltpu.VMEM((4, 4, 2, 32, 256), BF16),
        pltpu.VMEM((4, 2, 32, 256), BF16),
        pltpu.VMEM((4, 2, 32, 256), BF16),
        pltpu.VMEM((8, 8, 256), F32),
        pltpu.VMEM((8, 8, 256), F32),
        pltpu.VMEM((32, 128), F32),
        pltpu.VMEM((2, 32, 128), F32),
        pltpu.VMEM((4, 2, 32, 128), F32),
        pltpu.VMEM((3, 32, 128), F32),
        pltpu.VMEM((32, 128), F32),
        pltpu.VMEM((16, 32, 128), F32),
        pltpu.VMEM((8, 32, 128), F32),
    ]
    scratch += [dma((len(CONSTS),))]
    for n in (8, 31, 31, 3, 8):
        scratch += [dma((3, n)), dma((3, n))]
    for n in (7, 3, 3, 1, 7, 3, 3, 1, 1, 3, 1, 15, 7):
        scratch += [dma((n,)), dma((n,))]
    out_shape = (
        jax.ShapeDtypeStruct((2,) + latents.shape, BF16),
        jax.ShapeDtypeStruct((2, 4, 256), F32),
        jax.ShapeDtypeStruct((2, 2, 32, 32), F32),
    )
    outs = pl.pallas_call(
        kernel,
        out_shape=out_shape,
        in_specs=[hbm] + [vmem] * 5 + [hbm] * (1 + len(CONSTS)),
        out_specs=(hbm,) + (vmem,) * 2,
        scratch_shapes=scratch,
        compiler_params=pltpu.CompilerParams(
            collective_id=0, has_side_effects=True, vmem_limit_bytes=62 * 1024 * 1024
        ),
        name="spectral_block",
    )(
        latents,
        norm_gain.reshape(1, 256),
        weight_in,
        weight_out,
        filter_first.reshape(2, 32, 32),
        filter_second.reshape(2, 32, 32),
        cotangent,
        *consts,
    )
    fields, weights, filters = outs
    filters = filters.reshape(2, 2, 1, 32, 32)
    return fields[0], fields[1], weights[0], weights[1], filters[0], filters[1]


def solution(mesh):
    placed = (
        P("pen", "chan", None),
        P(),
        P(("pen", "chan"), None),
        P(("pen", "chan"), None),
        P(None, "chan", None, None),
        P(None, "chan", None, None),
        P("pen", "chan", None),
    )
    return jax.shard_map(
        body,
        mesh=mesh,
        in_specs=placed,
        out_specs=(
            P("pen", "chan", None),
            P("pen", "chan", None),
            P(("pen", "chan"), None),
            P(("pen", "chan"), None),
            P(None, "chan", None, None),
            P(None, "chan", None, None),
        ),
        check_vma=False,
    )
```
